32 devices in a mesh: groups: 2 (over x), attn: 8 (over z, y), expert: 2 (over core).
Axes of the slice: x: 2, y: 2, z: 4, core: 2. Of those that a mesh axis runs over, the one named last changes fastest.
Arguments:
- queries: bfloat16 [512, 6144], P(('groups', 'attn'), 'expert'), parts along dimension 0, may hold values from -128 to 128
- new_kv: bfloat16 [512, 2048], P(('groups', 'attn'), 'expert'), parts along dimension 0, may hold values from -16 to 16
- kv_pool: bfloat16 [1152, 16, 2048], P(('groups', 'attn'), None, 'expert'), parts along dimension 0, may hold values from -16 to 16
- page_counts: int32 [16, 32], P(('groups', 'attn')), parts along dimension 0, may hold values from 1 to 8, 72 in all within a row
- tail_tokens: int32 [512], P(('groups', 'attn')), parts along dimension 0, may hold values from 1 to 16
- page_order: int32 [16, 72], P(('groups', 'attn')), parts along dimension 0, may hold values from 0 to 71, each once within a row
- residual: bfloat16 [512, 6144], P(('groups', 'attn'), 'expert'), parts along dimension 0, may hold values from -100 to 100
- norm_gain: float32 [6144], P('expert'), may hold values from 0.5 to 1.5
- routes: int32 [512, 2], P(('groups', 'attn')), parts along dimension 0, may hold values from 0 to 7, as said below
- route_gates: float32 [512, 2], P(('groups', 'attn')), parts along dimension 0, may hold values from 0.2 to 0.8
- w_gate: bfloat16 [2, 6144, 2048], P('expert', None, 'attn'), may hold values from -0.078125 to 0.078125
- w_up: bfloat16 [2, 6144, 2048], P('expert', None, 'attn'), may hold values from -0.078125 to 0.078125
- w_down: bfloat16 [2, 2048, 6144], P('expert', 'attn'), may hold values from -0.125 to 0.125
- mig_pages: int32 [16, 2], P(('groups', 'attn')), parts along dimension 0, may hold values from 0 to 71, as said below
- mig_dest: int32 [16, 2], P(('groups', 'attn')), parts along dimension 0, may hold values from -1 to 7, as said below
Outputs:
- layer_out: bfloat16 [512, 6144], P(('groups', 'attn'), 'expert'), parts along dimension 0
- arrived: bfloat16 [32, 16, 2048], P(('groups', 'attn'), None, 'expert'), parts along dimension 0
The draws below stay inside these ranges and needn't reach their ends.
There are 2 independent parts, one for each index of `groups`. The reference program is written for one: setup_inputs(seed, part) draws one part's arguments, and reference() takes and returns one part's arrays. A program takes and returns all parts, laid end to end along the dimension named above; an argument that names none is the same for every part. Nothing has to cross between parts.
Inputs may be any that keep to these rules, and one draw needn't show every extreme that they name: `page_counts`: row a gives the pages of the 32 requests of attn index a and sums to 72. `page_order`: each row orders its 72 pages. `routes`: each row names two different experts; of the 32 rows of one attn index, each expert below 2 is named by at most 12 rows, and by exactly 12 rows at some attn index. `mig_pages`: the pages of one row differ. `mig_dest`: a row names each attn index at most once; an attn index is named by at most 2 entries in all, and one by exactly 2.
All inputs are finite; a program needn't handle non-finite values.
Results may differ from the reference program's by a relative error of at most 0.0045.
Values may be sent and summed in bfloat16 or wider, within the bound.
No kernel may reach another device: no remote copies, remote signals or barrier semaphores. Data moves between devices by JAX's collectives and lax.ppermute only.
A program may use at most 128 MiB of HBM per device.

```python
import math
import jax
import jax.numpy as jnp
import numpy as np
from jax import lax

D = 6144
H = 48
KVH = 8
HD = 128
EXPERTS = 8
FF_DEV = 256
PAGE = 16
MAXP = 8
REQ_DEV = 32
HOSTED = 2
FF = 2048
REQS = 256
CAP = 12
POOL = 72
POOLS = 576
MIGB = 2
N_ATTN = 8


def make_cache(key, lead):
    key_a, key_b = jax.random.split(key, 2)
    keys_part = jnp.clip(jax.random.normal(key_a, lead + (KVH, 1, HD), jnp.float32), -5.0, 5.0)
    values_part = jnp.clip(jax.random.normal(key_b, lead + (KVH, 1, HD), jnp.float32), -5.0, 5.0)
    return jnp.concatenate([keys_part, values_part], axis=-2)


def draw_queries(key, part):
    key = jax.random.fold_in(key, 17)
    key_a = jax.random.fold_in(key, 0)
    drawn = jnp.clip(jax.random.normal(key_a, (REQS, KVH, H // KVH, HD), jnp.float32), -5.0, 5.0)
    return drawn.reshape(REQS, H * HD).astype(jnp.bfloat16)


def draw_kv_pool(key, part):
    key = jax.random.fold_in(key, 19)
    made = make_cache(key, (POOLS, PAGE))
    return made.reshape(POOLS, PAGE, KVH * 2 * HD).astype(jnp.bfloat16)


def draw_new_kv(key, part):
    key = jax.random.fold_in(key, 23)
    made = make_cache(key, (REQS,))
    return made.reshape(REQS, KVH * 2 * HD).astype(jnp.bfloat16)


def draw_residual(key, part):
    key = jax.random.fold_in(key, 13)
    key_a, key_b, key_c = jax.random.split(key, 3)
    noise = jnp.clip(jax.random.normal(key_a, (REQS, D), jnp.float32), -5.0, 5.0)
    ramp = jnp.sqrt(1.0 + 2.0 * jnp.arange(D, dtype=jnp.float32) / (D - 1))[None, :]
    row_scale = jnp.exp(jax.random.uniform(key_b, (REQS, 1), jnp.float32, math.log(0.3), math.log(3.0)))
    col_scale = jnp.exp(jax.random.uniform(key_c, (1, D), jnp.float32, math.log(0.7), math.log(1.4)))
    made = noise * row_scale * col_scale * ramp
    return made.astype(jnp.bfloat16)


def draw_routes(key, part):
    key = jax.random.fold_in(key, 5)
    key_a, key_b, key_c, key_d, key_e = jax.random.split(key, 5)
    lowest = max(1, CAP // 3)
    loads = jax.random.randint(key_a, (N_ATTN, 2), lowest, CAP + 1)
    forced = jax.random.randint(key_b, (2,), 0, N_ATTN)
    loads = jnp.where(jnp.arange(N_ATTN)[:, None] == forced[None, :], CAP, loads)
    ranking = jax.random.randint(key_c, (N_ATTN, 2, REQ_DEV), 0, 1 << 20) * REQ_DEV + jnp.arange(REQ_DEV)
    ranks = jnp.argsort(jnp.argsort(ranking, axis=2), axis=2)
    member = ranks < loads[:, :, None]
    first_in = member[:, 0]
    second_in = member[:, 1]
    others = EXPERTS - 2
    other_a = jax.random.randint(key_d, (N_ATTN, REQ_DEV), 0, others)
    other_b = (other_a + jax.random.randint(key_e, (N_ATTN, REQ_DEV), 1, others)) % others
    other_a = other_a + 2
    other_b = other_b + 2
    column_one = jnp.where(first_in, 0, jnp.where(second_in, 1, other_a))
    column_two = jnp.where(first_in & second_in, 1, jnp.where(first_in | second_in, other_a, other_b))
    return jnp.stack([column_one, column_two], axis=-1).reshape(REQS, 2).astype(jnp.int32)


def draw_mig_pages(key, part):
    key = jax.random.fold_in(key, 7)
    ranking = jax.random.randint(key, (N_ATTN, POOL), 0, 1 << 20) * POOL + jnp.arange(POOL)
    return jnp.argsort(ranking, axis=1)[:, :MIGB].astype(jnp.int32)


def draw_mig_dest(key, part):
    key = jax.random.fold_in(key, 9)
    key_a, key_b, key_c = jax.random.split(key, 3)
    spread_order = jnp.argsort(jax.random.randint(key_a, (N_ATTN,), 0, 1 << 20) * N_ATTN + jnp.arange(N_ATTN))
    offsets = spread_order[:MIGB]
    naming = jnp.argsort(jax.random.randint(key_b, (N_ATTN,), 0, 1 << 20) * N_ATTN + jnp.arange(N_ATTN))
    target = (jnp.arange(N_ATTN)[:, None] + offsets[None, :]) % N_ATTN
    live = (jax.random.randint(key_c, (N_ATTN, MIGB), 0, 2) == 1) | (target == 0)
    return jnp.where(live, naming[target], -1).astype(jnp.int32)


def with_ends(result, own_key, smallest, top_value):
    longest = result.shape.index(max(result.shape))
    spots = []
    for shift in (0, 1):
        where = [jax.random.randint(jax.random.fold_in(own_key, axis), (), 0, length) for axis, length in enumerate(result.shape)]
        where[longest] = (where[longest] + shift) % result.shape[longest]
        spots.append(tuple(where))
    return result.at[spots[0]].set(smallest).at[spots[1]].set(top_value)


def steps_of(rng, dims, shards, smallest, largest):
    def one(dim, parts):
        draws = jax.random.uniform(jax.random.fold_in(jax.random.fold_in(rng, 6), dim), (parts,), jnp.float32, smallest / len(shards), largest / len(shards))
        return jnp.repeat(jnp.exp(draws), dims[dim] // parts).reshape((-1,) + (1,) * (len(dims) - dim - 1))

    level = one(*shards[0])
    for cut in shards[1:]:
        level = level * one(*cut)
    return level


def length_profile(amount, total, most, slope):
    weights = [(1 << 20) // math.isqrt(standing ** slope) + 1 for standing in range(2, amount + 1)]
    rest, given = total - most - (amount - 1), [1] * (amount - 1)
    while rest > 0:
        movable = [i for i in range(amount - 1) if given[i] < most]
        mass, left = sum([weights[i] for i in movable]), rest
        for i in movable:
            more = min(most - given[i], max(1, left * weights[i] // mass), rest)
            given[i] = given[i] + more
            rest = rest - more
    return np.array([most] + given)


def uneven(rng, count, total, limit, skew):
    if count == 2:
        one = jax.random.randint(rng, (), max(1, total - limit), min(limit, total - 1) + 1)
        return jnp.stack([one, total - one])
    sizes = jnp.asarray(length_profile(count, total, limit, skew), jnp.int32)
    couples = (count - 1) // 2
    giver, receiver = sizes[1:1 + 2 * couples:2], sizes[2:2 + 2 * couples:2]
    margin = jnp.minimum(giver - 1, limit - receiver)
    passed = jax.random.randint(jax.random.fold_in(rng, 1), (couples,), 0, 1 << 20) % (margin + 1)
    sizes = sizes.at[1:1 + 2 * couples:2].set(giver - passed).at[2:2 + 2 * couples:2].set(receiver + passed)
    return sizes[jax.random.permutation(jax.random.fold_in(rng, 2), count)]


def scatter_about(key, shape, width, limit, pieces=(), kind=jnp.bfloat16):
    entries = jax.random.normal(key, shape, jnp.float32) * width
    if len(pieces) > 0:
        entries = steps_of(key, shape, pieces, -0.22, 0.18) * entries
    return jnp.clip(entries, min=-limit, max=limit).astype(kind)


def setup_inputs(seed: int = 0, part: int = 0) -> dict:
    key_list = jax.random.split(jax.random.key(seed), 16)
    part_keys = jax.random.split(jax.random.fold_in(key_list[15], part), 16)
    return {
        "queries": draw_queries(jax.random.fold_in(jax.random.fold_in(key_list[15], part), 71), part),
        "new_kv": draw_new_kv(jax.random.fold_in(jax.random.fold_in(key_list[15], part), 71), part),
        "kv_pool": draw_kv_pool(jax.random.fold_in(jax.random.fold_in(key_list[15], part), 71), part),
        "page_counts": jax.vmap(lambda own: uneven(own, REQ_DEV, POOL, MAXP, 2))(jax.random.split(part_keys[3], N_ATTN)).reshape((N_ATTN, REQ_DEV)).astype(jnp.int32),
        "tail_tokens": with_ends(jax.random.randint(part_keys[4], (REQS,), 1, PAGE + 1), jax.random.fold_in(part_keys[4], 1), 1, PAGE).astype(jnp.int32),
        "page_order": jax.vmap(lambda own: jax.random.permutation(own, POOL))(jax.random.split(part_keys[5], N_ATTN)).reshape((N_ATTN, POOL)).astype(jnp.int32),
        "residual": draw_residual(jax.random.fold_in(jax.random.fold_in(key_list[15], part), 71), part),
        "norm_gain": jnp.clip(1.0 + 0.1 * jax.random.normal(key_list[7], (D,), jnp.float32), 0.5, 1.5),
        "routes": draw_routes(jax.random.fold_in(jax.random.fold_in(key_list[15], part), 71), part),
        "route_gates": jnp.clip(0.2 + 0.6 * jax.random.uniform(part_keys[9], (REQS, 2), jnp.float32) ** steps_of(part_keys[9], (REQS, 2), ((0, 8),), -0.2, 0.2), 0.2, 0.8),
        "w_gate": scatter_about(key_list[10], (HOSTED, D, FF), D ** -0.5, 0.078125, ((0, 2), (2, 8))),
        "w_up": scatter_about(key_list[11], (HOSTED, D, FF), D ** -0.5, 0.078125, ((0, 2), (2, 8))),
        "w_down": scatter_about(key_list[12], (HOSTED, FF, D), FF ** -0.5, 0.125, ((0, 2), (1, 8))),
        "mig_pages": draw_mig_pages(jax.random.fold_in(jax.random.fold_in(key_list[15], part), 71), part),
        "mig_dest": draw_mig_dest(jax.random.fold_in(jax.random.fold_in(key_list[15], part), 71), part),
    }


EPSILON = 1e-05
HIGHEST = lax.Precision.HIGHEST

def attend_index(operands):
    query_rows, fresh_rows, pool_pages, counts, tail_counts, order_row = operands
    offsets = jnp.cumsum(counts) - counts
    slot_ids = jnp.minimum(offsets[:, None] + jnp.arange(MAXP, dtype=jnp.int32)[None, :], POOL - 1)
    page_ids = jnp.take(order_row, slot_ids, axis=0)
    cached = jnp.take(pool_pages, page_ids.reshape(-1), axis=0)
    cached = cached.reshape(REQ_DEV, MAXP * PAGE, KVH, 2, HD).astype(jnp.float32)
    lengths = (counts - 1) * PAGE + tail_counts
    query_heads = query_rows.reshape(REQ_DEV, KVH, H // KVH, HD).astype(jnp.float32)
    newest = fresh_rows.reshape(REQ_DEV, KVH, 2, HD).astype(jnp.float32)
    score_scale = HD ** (-0.5)
    scores = jnp.einsum('rkgd,rtkd->rkgt', query_heads, cached[:, :, :, 0], precision=HIGHEST) * score_scale
    own_score = jnp.einsum('rkgd,rkd->rkg', query_heads, newest[:, :, 0], precision=HIGHEST) * score_scale
    in_range = (jnp.arange(MAXP * PAGE, dtype=jnp.int32)[None, :] < lengths[:, None])[:, None, None, :]
    row_top = jnp.maximum(lax.optimization_barrier(jnp.max(jnp.where(in_range, scores, -jnp.inf), axis=-1)), own_score)
    weights = jnp.where(in_range, jnp.exp(scores - row_top[..., None]), 0.0)
    own_weight = jnp.exp(own_score - row_top)
    denominator = lax.optimization_barrier(jnp.sum(weights, axis=-1)) + own_weight
    probabilities = lax.optimization_barrier((weights / denominator[..., None]).astype(jnp.bfloat16)).astype(jnp.float32)
    own_prob = lax.optimization_barrier((own_weight / denominator).astype(jnp.bfloat16)).astype(jnp.float32)
    mixed_heads = jnp.einsum('rkgt,rtkd->rkgd', probabilities, cached[:, :, :, 1], precision=HIGHEST)
    mixed_heads = mixed_heads + own_prob[..., None] * newest[:, :, 1][:, :, None, :]
    return mixed_heads.reshape(REQ_DEV, D)

def add_share(total, pair):
    act_block, down_block = pair
    part_sum = jnp.dot(act_block, down_block, preferred_element_type=jnp.float32)
    part_sum = lax.optimization_barrier(part_sum.astype(jnp.bfloat16)).astype(jnp.float32)
    return (total + part_sum, None)

def reference(queries, new_kv, kv_pool, page_counts, tail_tokens, page_order, residual, norm_gain, routes, route_gates, w_gate, w_up, w_down, mig_pages, mig_dest):
    attended = lax.map(attend_index, (queries.reshape(N_ATTN, REQ_DEV, H * HD), new_kv.reshape(N_ATTN, REQ_DEV, KVH * 2 * HD), kv_pool.reshape(N_ATTN, POOL, PAGE, KVH * 2 * HD), page_counts, tail_tokens.reshape(N_ATTN, REQ_DEV), page_order)).reshape(REQS, D)
    hidden = residual.astype(jnp.float32) + attended
    squares = lax.optimization_barrier(jnp.sum(hidden * hidden, axis=1, keepdims=True))
    normed = (hidden * lax.rsqrt(squares / D + EPSILON) * norm_gain).astype(jnp.bfloat16)
    slot_iota = jnp.arange(CAP, dtype=jnp.int32)
    grouped_routes = routes.reshape(N_ATTN, REQ_DEV, 2)
    grouped_gates = route_gates.reshape(N_ATTN, REQ_DEV, 2)
    grouped_rows = normed.reshape(N_ATTN, REQ_DEV, D).astype(jnp.float32)
    moe_total = jnp.zeros((N_ATTN, REQ_DEV, D), jnp.float32)
    for expert in range(HOSTED):
        chosen = grouped_routes == expert
        member = jnp.any(chosen, axis=2)
        gate_share = lax.optimization_barrier(jnp.sum(jnp.where(chosen, grouped_gates, 0.0), axis=2))
        slot_rank = jnp.cumsum(member.astype(jnp.int32), axis=1) - 1
        onehot = ((slot_rank[:, None, :] == slot_iota[None, :, None]) & member[:, None, :]).astype(jnp.float32)
        slot_rows = jnp.einsum('ncr,nrd->ncd', onehot, grouped_rows, precision=HIGHEST).astype(jnp.bfloat16)
        slot_rows = slot_rows.reshape(N_ATTN * CAP, D)
        gate_value = jnp.dot(slot_rows, w_gate[expert], preferred_element_type=jnp.float32)
        up_value = jnp.dot(slot_rows, w_up[expert], preferred_element_type=jnp.float32)
        active = (jax.nn.silu(gate_value) * up_value).astype(jnp.bfloat16)
        active_blocks = jnp.moveaxis(active.reshape(N_ATTN * CAP, N_ATTN, FF_DEV), 1, 0)
        down_blocks = w_down[expert].reshape(N_ATTN, FF_DEV, D)
        summed, unused = lax.scan(add_share, jnp.zeros((N_ATTN * CAP, D), jnp.float32), (active_blocks, down_blocks))
        expert_out = summed.astype(jnp.bfloat16)
        expert_out = expert_out.reshape(N_ATTN, CAP, D).astype(jnp.float32)
        moe_total = moe_total + jnp.einsum('ncr,ncd->nrd', onehot * gate_share[:, None, :], expert_out, precision=HIGHEST)
    layer_out = (hidden + moe_total.reshape(REQS, D)).astype(jnp.bfloat16)
    source_ids = jnp.repeat(jnp.arange(N_ATTN, dtype=jnp.int32), MIGB)
    flat_dest = mig_dest.reshape(-1)
    global_pages = source_ids * POOL + mig_pages.reshape(-1)
    payload = jnp.take(kv_pool, global_pages, axis=0)
    live = flat_dest >= 0
    earlier = (flat_dest[None, :] == flat_dest[:, None]) & live[None, :] & (source_ids[None, :] < source_ids[:, None])
    arrival_rank = lax.optimization_barrier(jnp.sum(earlier.astype(jnp.int32), axis=1))
    target_rows = jnp.where(live, flat_dest * MIGB + arrival_rank, N_ATTN * MIGB)
    arrived = jnp.zeros((N_ATTN * MIGB, PAGE, KVH * 2 * HD), jnp.bfloat16).at[target_rows].set(payload, mode='drop')
    return (layer_out, arrived)
```

```python
import functools

import jax
import jax.numpy as jnp
from jax import lax
from jax.experimental import pallas as pl
from jax.experimental.pallas import tpu as pltpu
from jax.sharding import PartitionSpec as P

D = 6144
HD = 128
PAGE = 16
CAP = 12
EPSILON = 1e-05
HALF = D // 2
QUARTER = D // 4
LO = 8
SLOT_COLS = HALF + QUARTER
LANES = 128
SCORE_SCALE = HD ** (-0.5)
NEG = -1e30
F32 = jnp.float32
BF16 = jnp.bfloat16
VMEM = pl.BlockSpec(memory_space=pltpu.VMEM)
SMEM = pl.BlockSpec(memory_space=pltpu.SMEM)
ANY = pl.BlockSpec(memory_space=pl.ANY)


def iota(shape, dim):
    return lax.broadcasted_iota(jnp.int32, shape, dim)


def eye(size):
    return iota((size, size), 0) == iota((size, size), 1)


def to_column(row, size):
    return jnp.sum(jnp.where(eye(size), row, 0.0), axis=1, keepdims=True)


def to_row(column, size):
    return jnp.sum(jnp.where(eye(size), column, 0.0), axis=0, keepdims=True)


def dot(a, b):
    return lax.dot_general(a, b, (((1,), (0,)), ((), ())), preferred_element_type=F32)


def dot_t(a, b):
    return lax.dot_general(a, b, (((1,), (1,)), ((), ())), preferred_element_type=F32)


def members(routes, expert):
    chosen = (routes[:, 0:1] == expert) | (routes[:, 1:2] == expert)
    return jnp.where(chosen, 1.0, 0.0)


def mix_slots(shape, dim, part):
    index = iota(shape, dim)
    here = (index >= 4 * part) & (index < 4 * part + 4)
    return jnp.where(here, index - 4 * part + LO, -1).astype(F32)


def split_three(value):
    high = value.astype(BF16)
    rest = value - high.astype(F32)
    middle = rest.astype(BF16)
    low = (rest - middle.astype(F32)).astype(BF16)
    return high.astype(F32), middle.astype(F32), low.astype(F32)


def attend_kernel(
    hosted, queries, new_kv, pool, counts, tails, order, residual, gain, routes, mig_pages, mig_dest, hidden, slots, moved
):
    rows = queries.shape[0]
    tokens = pool.shape[0]
    pages = tokens // PAGE
    heads_here = pool.shape[1] // (2 * HD)
    group = queries.shape[1] // (heads_here * HD)
    width = queries.shape[1]

    counts_row = counts[...].astype(F32)
    row_a, row_b = iota((rows, rows), 0), iota((rows, rows), 1)
    first = jnp.sum(jnp.where(row_b < row_a, counts_row, 0.0), axis=1, keepdims=True)
    count = to_column(counts_row, rows)
    tail = to_column(tails[...].astype(F32), rows)
    place = iota((rows, pages), 1).astype(F32)
    inside = (place >= first) & (place < first + count)
    held = jnp.where(inside, jnp.where(place == first + count - 1.0, tail, float(PAGE)), 0.0)
    page_at = to_column(order[...].astype(F32), pages)
    page_of = (iota((pages, tokens), 1) // PAGE).astype(F32)
    placed = jnp.where(page_at == page_of, 1.0, 0.0).astype(BF16)
    limit = dot(held.astype(BF16), placed)
    visible = (iota((rows, tokens), 1) % PAGE).astype(F32) < limit
    penalty = jnp.where(visible, 0.0, NEG)[None]
    own_penalty = jnp.where(eye(rows), 0.0, NEG)[None]

    squares = jnp.zeros((rows, HD), F32)
    for head in range(heads_here):
        base = head * group * HD
        query = jnp.concatenate(
            [queries[:, base + g * HD : base + (g + 1) * HD] for g in range(group)], axis=0
        )
        key_at, value_at = 2 * head * HD, (2 * head + 1) * HD
        scores = dot_t(query, pool[:, key_at : key_at + HD]) * SCORE_SCALE
        own = dot_t(query, new_kv[:, key_at : key_at + HD]) * SCORE_SCALE
        scores = (scores.reshape(group, rows, tokens) + penalty).reshape(group * rows, tokens)
        own = (own.reshape(group, rows, rows) + own_penalty).reshape(group * rows, rows)
        top = jnp.maximum(
            jnp.max(scores, axis=1, keepdims=True), jnp.max(own, axis=1, keepdims=True)
        )
        weights = jnp.exp(scores - top)
        own_weights = jnp.exp(own - top)
        total = jnp.sum(weights, axis=1, keepdims=True) + jnp.sum(own_weights, axis=1, keepdims=True)
        inverse = 1.0 / total
        mixed = dot((weights * inverse).astype(BF16), pool[:, value_at : value_at + HD])
        mixed = mixed + dot((own_weights * inverse).astype(BF16), new_kv[:, value_at : value_at + HD])
        for g in range(group):
            columns = slice(base + g * HD, base + (g + 1) * HD)
            part = residual[:, columns].astype(F32) + mixed[g * rows : (g + 1) * rows]
            hidden[:, columns] = part
            squares = squares + part * part
    square_row = to_row(jnp.sum(squares, axis=1, keepdims=True), rows)

    scaled = (hidden[...] * gain[...]).astype(BF16)
    lows, mixes = [], []
    for expert in range(hosted):
        member = members(routes[...], expert)
        member_row = to_row(member, rows)
        rank = jnp.sum(jnp.where(row_a <= row_b, member, 0.0), axis=0, keepdims=True) - 1.0
        rank = jnp.where(member_row > 0.0, rank, -2.0)
        lows.append(rank == iota((LO, rows), 0).astype(F32))
        mixes.append([rank == mix_slots((LO, rows), 0, part) for part in range(2)])
    picked = []
    for part in range(2):
        maps = [jnp.where(m, 1.0, 0.0) for m in lows] + [jnp.where(m[part], 1.0, 0.0) for m in mixes]
        stacked = jnp.concatenate(maps, axis=0).astype(BF16)
        picked.append(dot(stacked, scaled[:, part * QUARTER : (part + 1) * QUARTER]))
    lane = iota((LO, LANES), 1)
    for expert in range(hosted):
        low_at, mix_at = expert * LO, (hosted + expert) * LO
        low_sum = jnp.sum(jnp.where(lows[expert], square_row, 0.0), axis=1, keepdims=True)
        mix_map = mixes[expert][0] | mixes[expert][1]
        mix_sum = jnp.sum(jnp.where(mix_map, square_row, 0.0), axis=1, keepdims=True)
        extra = jnp.zeros((LO, LANES), F32)
        for at, piece in enumerate(split_three(low_sum) + split_three(mix_sum)):
            extra = jnp.where(lane == at, piece, extra)
        for part in range(2):
            columns = slice(part * QUARTER, (part + 1) * QUARTER)
            slots[expert, :, columns] = picked[part][low_at : low_at + LO].astype(BF16)
        mixed_rows = picked[0][mix_at : mix_at + LO] + picked[1][mix_at : mix_at + LO]
        slots[expert, :, HALF:SLOT_COLS] = mixed_rows.astype(BF16)
        slots[expert, :, SLOT_COLS:] = extra.astype(BF16)

    entries = mig_pages.shape[1]
    page_width = pool.shape[1]
    lane = iota((PAGE, LANES), 1)
    notes = jnp.where(lane == entries, lax.axis_index("attn").astype(F32), 0.0)
    for entry in range(entries):
        start = pl.multiple_of(mig_pages[0, entry] * PAGE, PAGE)
        moved[:, entry * page_width : (entry + 1) * page_width] = pool[pl.ds(start, PAGE), :]
        notes = jnp.where(lane == entry, mig_dest[0, entry].astype(F32), notes)
    moved[:, entries * page_width :] = notes.astype(BF16)


def pack_kernel(mine, theirs, moved, message):
    lane = iota((LO, LANES), 1)
    extra = mine[:, SLOT_COLS:].astype(F32) + theirs[:, SLOT_COLS:].astype(F32)
    low_scale = lax.rsqrt(jnp.sum(jnp.where(lane < 3, extra, 0.0), axis=1, keepdims=True) / D + EPSILON)
    mix_sum = jnp.sum(jnp.where((lane >= 3) & (lane < 6), extra, 0.0), axis=1, keepdims=True)
    mix_scale = lax.rsqrt(mix_sum / D + EPSILON)
    first_half = lax.axis_index("expert") == 0
    for columns, scale in ((slice(0, HALF), low_scale), (slice(HALF, SLOT_COLS), mix_scale)):
        a = mine[:, columns].astype(F32) * scale
        b = theirs[:, columns].astype(F32) * scale
        both = jnp.concatenate([jnp.where(first_half, a, b), jnp.where(first_half, b, a)], axis=0)
        message[:, columns] = both.astype(BF16)
    message[:, SLOT_COLS:] = moved[...]


def ffn_kernel(n, cut, *refs):
    blocks, (gate_hbm, up_hbm, down_hbm) = refs[: n + 1], refs[n + 1 : n + 4]
    outs = refs[n + 4 : 2 * n + 4]
    low_rows, mix_rows, gate, up, down, gate_sum, up_sum, sems = refs[2 * n + 4 :]
    copies = []
    for q in range(4):
        part = pl.ds(q * QUARTER, QUARTER)
        copies.append(pltpu.make_async_copy(gate_hbm.at[part, :], gate.at[part, :], sems.at[0, q]))
        copies.append(pltpu.make_async_copy(up_hbm.at[part, :], up.at[part, :], sems.at[1, q]))
    for q in range(4):
        part = pl.ds(q * QUARTER, QUARTER)
        copies.append(pltpu.make_async_copy(down_hbm.at[:, part], down.at[:, part], sems.at[2, q]))
    for copy in copies:
        copy.start()
    for j in range(n - 1):
        low_rows[16 * j : 16 * j + 16, :] = blocks[j][:, :HALF]
        mix_rows[16 * j : 16 * j + 16, :] = blocks[j][:, HALF:SLOT_COLS]
    j = n - 1
    low_rows[16 * j : 16 * j + 16, :] = blocks[j][:, :HALF]
    mix_rows[16 * j : 16 * j + 16, : cut - HALF] = blocks[j][:, HALF:cut]
    mix_rows[16 * j : 16 * j + 16, cut - HALF :] = blocks[n][:, : SLOT_COLS - cut]

    size = min(n, 8)
    span = 16 * size
    row = iota((span, 1), 0) % 16
    for q in range(4):
        copies[2 * q].wait()
        copies[2 * q + 1].wait()
        low_here, mix_here = (row // 8) == q // 2, (row // 4) == q
        part = slice(q * QUARTER, (q + 1) * QUARTER)
        within = slice((q % 2) * QUARTER, (q % 2 + 1) * QUARTER)
        for at in range(0, 16 * n, span):
            left = jnp.concatenate([low_rows[at : at + span, within], mix_rows[at : at + span, :]], axis=0)
            for weight, total in ((gate, gate_sum), (up, up_sum)):
                product = dot(left, weight[part, :])
                low = jnp.where(low_here, product[:span], 0.0)
                mix = jnp.where(mix_here, product[span:], 0.0)
                if q == 0:
                    total[0, at : at + span, :] = low
                    total[1, at : at + span, :] = mix
                else:
                    total[0, at : at + span, :] += low
                    total[1, at : at + span, :] += mix

    for copy in copies[8:]:
        copy.wait()
    lower = iota((8 * size, 1), 0) % 8 < 4
    width = gate.shape[1]

    def fold(total, at):
        low, mix = [
            jnp.sum(total[k, at : at + span, :].reshape(size, 2, 8, width), axis=1).reshape(8 * size, width)
            for k in range(2)
        ]
        other = jnp.where(lower, pltpu.roll(mix, 8 * size - 4, 0), pltpu.roll(mix, 4, 0))
        return low, mix + other

    first_rows = iota((8, 1), 0) < 4
    for at in range(0, 16 * n, span):
        pieces = [jax.nn.silu(g) * u for g, u in zip(fold(gate_sum, at), fold(up_sum, at))]
        active = jnp.concatenate([p.reshape(size, 8, width) for p in pieces], axis=1)
        active = active.reshape(span, width).astype(BF16)
        quarters = [dot(active, down[:, q * QUARTER : (q + 1) * QUARTER]) for q in range(4)]
        for j in range(size):
            out = outs[at // 16 + j]
            low_at, mix_at = slice(16 * j, 16 * j + 8), slice(16 * j + 8, 16 * j + 16)
            for part in range(2):
                both = jnp.concatenate([quarters[part][low_at], quarters[2 + part][low_at]], axis=0)
                out[:, part * QUARTER : (part + 1) * QUARTER] = both.astype(BF16)
            both = jnp.concatenate(
                [jnp.where(first_rows, quarters[k][mix_at], quarters[k + 1][mix_at]) for k in (0, 2)], axis=0
            )
            out[:, HALF:] = both.astype(BF16)


def arrive_kernel(n, cut, page_width, *refs):
    blocks, arrived, board, board_smem, sem = refs[: n + 1], refs[n + 1], refs[n + 2], refs[n + 3], refs[n + 4]
    entries = arrived.shape[0]
    notes_at = SLOT_COLS + entries * page_width
    heads = [block[:, notes_at:].astype(F32)[0:1] for block in blocks[: n - 1]]
    heads.append(blocks[n][:, notes_at - cut :].astype(F32)[0:1])
    notes = jnp.concatenate(heads, axis=0)
    lane = iota((n, LANES), 1)
    match = (notes == lax.axis_index("attn").astype(F32)) & (lane < entries)
    named = jnp.max(jnp.where(match, 1.0, 0.0), axis=1, keepdims=True)
    source = jnp.sum(jnp.where(lane == entries, notes, 0.0), axis=1, keepdims=True)
    earlier = to_row(source, n) < source
    rank = jnp.sum(jnp.where(earlier, to_row(named, n), 0.0), axis=1, keepdims=True)
    board[...] = jnp.where(match, rank, -1.0).astype(jnp.int32)
    copy = pltpu.make_async_copy(board, board_smem, sem)
    copy.start()
    arrived[...] = jnp.zeros_like(arrived)
    copy.wait()
    for j in range(n):
        block, shift = (blocks[j], 0) if j < n - 1 else (blocks[n], cut)
        for entry in range(entries):
            slot = board_smem[j, entry]
            at = SLOT_COLS + entry * page_width - shift

            @pl.when(slot >= 0)
            def _():
                arrived[slot] = block[:, at : at + page_width]


def finish_kernel(own, from_left, from_right, mine, other):
    total = own[...].astype(F32) + from_left[...].astype(F32) + from_right[...].astype(F32)
    first_half = lax.axis_index("expert") == 0
    top, bottom = total[:LO], total[LO:]
    mine[...] = jnp.where(first_half, top, bottom).astype(BF16)
    other[...] = jnp.where(first_half, bottom, top).astype(BF16)


def combine_kernel(hosted, hidden, mine, theirs, routes, gates, layer_out):
    rows = hidden.shape[0]
    first_half = lax.axis_index("expert") == 0
    a, b = mine[...].astype(F32), theirs[...].astype(F32)
    by_expert = [jnp.where(first_half, a, b).astype(BF16), jnp.where(first_half, b, a).astype(BF16)]
    row_a, row_b = iota((rows, rows), 0), iota((rows, rows), 1)
    terms = [[], []]
    for expert in range(hosted):
        member = members(routes[...], expert)
        share = jnp.sum(jnp.where(routes[...] == expert, gates[...], 0.0), axis=1, keepdims=True)
        rank = jnp.sum(jnp.where(row_b <= row_a, to_row(member, rows), 0.0), axis=1, keepdims=True) - 1.0
        rank = jnp.where(member > 0.0, rank, -2.0)
        low = jnp.where(rank == iota((rows, LO), 1).astype(F32), 1.0, 0.0).astype(BF16)
        for part in range(2):
            columns = slice(part * QUARTER, (part + 1) * QUARTER)
            mix = jnp.where(rank == mix_slots((rows, LO), 1, part), 1.0, 0.0).astype(BF16)
            value = dot(low, by_expert[expert][:, columns]) + dot(mix, by_expert[expert][:, HALF:])
            terms[part].append(share * value)
    for part in range(2):
        columns = slice(part * QUARTER, (part + 1) * QUARTER)
        layer_out[:, columns] = (hidden[:, columns] + (terms[part][0] + terms[part][1])).astype(BF16)


def call(kernel, outs, in_specs, args, scratch=(), flops=0, bytes_accessed=0, vmem=32 << 20):
    many = isinstance(outs, (list, tuple))
    return pl.pallas_call(
        kernel,
        out_shape=outs,
        in_specs=in_specs,
        out_specs=[VMEM] * len(outs) if many else VMEM,
        scratch_shapes=list(scratch),
        compiler_params=pltpu.CompilerParams(vmem_limit_bytes=vmem),
        cost_estimate=pl.CostEstimate(flops=flops, bytes_accessed=bytes_accessed, transcendentals=0),
    )(*args)


def ring_order(n):
    return [0, 2, 4, 6, 7, 5, 3, 1] if n == 8 else list(range(n))


def add(a, b):
    return (a.astype(F32) + b.astype(F32)).astype(BF16)


def per_device(
    n,
    hosted,
    queries,
    new_kv,
    kv_pool,
    page_counts,
    tail_tokens,
    page_order,
    residual,
    norm_gain,
    routes,
    route_gates,
    w_gate,
    w_up,
    w_down,
    mig_pages,
    mig_dest,
):
    rows, width = queries.shape
    page_width = kv_pool.shape[2]
    entries = mig_pages.shape[1]
    pool = kv_pool.reshape(-1, page_width)
    around = ring_order(n)
    right = [(around[i], around[(i + 1) % n]) for i in range(n)]
    left = [(b, a) for a, b in right]
    swap = [(0, 1), (1, 0)]
    shape = jax.ShapeDtypeStruct

    moved_cols = entries * page_width + LANES
    hidden, slots, moved = call(
        functools.partial(attend_kernel, hosted),
        [
            shape((rows, width), F32),
            shape((hosted, LO, SLOT_COLS + LANES), BF16),
            shape((PAGE, moved_cols), BF16),
        ],
        [VMEM] * 9 + [SMEM] * 2,
        (
            queries,
            new_kv,
            pool,
            page_counts,
            tail_tokens.reshape(1, -1),
            page_order,
            residual,
            norm_gain.reshape(1, -1),
            routes,
            mig_pages,
            mig_dest,
        ),
        flops=500_000_000,
        bytes_accessed=3_500_000,
    )

    own_expert = lax.axis_index("expert")
    mine = lax.dynamic_index_in_dim(slots, own_expert, 0, keepdims=False)
    other = lax.dynamic_index_in_dim(slots, 1 - own_expert, 0, keepdims=False)
    theirs = lax.ppermute(other, "expert", swap)
    cols = SLOT_COLS + moved_cols
    message = call(
        pack_kernel,
        shape((2 * LO, cols), BF16),
        [VMEM] * 3,
        (mine, theirs, moved),
        flops=500_000,
        bytes_accessed=500_000,
    )

    far = n // 2
    cut = HALF + 3 * LANES
    from_left, from_right = [message], [message]
    for _ in range(far - 1):
        from_left.append(lax.ppermute(from_left[-1], "attn", right))
        from_right.append(lax.ppermute(from_right[-1], "attn", left))
    last_a = lax.ppermute(from_left[-1][:, :cut], "attn", right)
    last_b = lax.ppermute(from_right[-1][:, cut:], "attn", left)
    blocks = [message] + from_left[1:] + from_right[1:] + [last_a, last_b]

    ff = w_gate.shape[2]
    size = 16 * n
    outs = call(
        functools.partial(ffn_kernel, n, cut),
        [shape((2 * LO, SLOT_COLS), BF16)] * n,
        [VMEM] * (n + 1) + [ANY] * 3,
        (*blocks, w_gate[0], w_up[0], w_down[0]),
        scratch=(
            pltpu.VMEM((size, HALF), BF16),
            pltpu.VMEM((size, QUARTER), BF16),
            pltpu.VMEM((D, ff), BF16),
            pltpu.VMEM((D, ff), BF16),
            pltpu.VMEM((ff, D), BF16),
            pltpu.VMEM((2, size, ff), F32),
            pltpu.VMEM((2, size, ff), F32),
            pltpu.SemaphoreType.DMA((3, 4)),
        ),
        flops=2_000_000_000,
        bytes_accessed=12_000_000,
        vmem=48 << 20,
    )
    arrived = call(
        functools.partial(arrive_kernel, n, cut, page_width),
        shape((entries, PAGE, page_width), BF16),
        [VMEM] * (n + 1),
        tuple(blocks),
        scratch=(
            pltpu.VMEM((n, LANES), jnp.int32),
            pltpu.SMEM((n, LANES), jnp.int32),
            pltpu.SemaphoreType.DMA,
        ),
        flops=100_000,
        bytes_accessed=2_000_000,
    )

    to_left = {k: outs[k] for k in range(1, far)}
    to_right = {k: outs[far - 1 + k] for k in range(1, far)}
    split = SLOT_COLS // 2
    going_right = lax.ppermute(outs[n - 1][:, :split], "attn", right)
    going_left = lax.ppermute(outs[n - 1][:, split:], "attn", left)
    for k in range(far - 1, 0, -1):
        if k == far - 1:
            send_right = jnp.concatenate([add(to_right[k][:, :split], going_right), to_right[k][:, split:]], axis=1)
            send_left = jnp.concatenate([to_left[k][:, :split], add(to_left[k][:, split:], going_left)], axis=1)
        else:
            send_right, send_left = add(to_right[k], going_right), add(to_left[k], going_left)
        going_right = lax.ppermute(send_right, "attn", right)
        going_left = lax.ppermute(send_left, "attn", left)
    kept, other_half = call(
        finish_kernel,
        [shape((LO, SLOT_COLS), BF16)] * 2,
        [VMEM] * 3,
        (outs[0], going_right, going_left),
        flops=500_000,
        bytes_accessed=600_000,
    )
    returned = lax.ppermute(other_half, "expert", swap)
    layer_out = call(
        functools.partial(combine_kernel, hosted),
        shape((rows, width), BF16),
        [VMEM] * 5,
        (hidden, kept, returned, routes, route_gates),
        flops=20_000_000,
        bytes_accessed=800_000,
    )
    return layer_out, arrived


def solution(mesh):
    n, hosted = mesh.shape["attn"], mesh.shape["expert"]
    return jax.shard_map(
        functools.partial(per_device, n, hosted),
        mesh=mesh,
        in_specs=(
            P(("groups", "attn"), "expert"),
            P(("groups", "attn"), "expert"),
            P(("groups", "attn"), None, "expert"),
            P(("groups", "attn"), None),
            P(("groups", "attn")),
            P(("groups", "attn"), None),
            P(("groups", "attn"), "expert"),
            P("expert"),
            P(("groups", "attn"), None),
            P(("groups", "attn"), None),
            P("expert", None, "attn"),
            P("expert", None, "attn"),
            P("expert", "attn", None),
            P(("groups", "attn"), None),
            P(("groups", "attn"), None),
        ),
        out_specs=(P(("groups", "attn"), "expert"), P(("groups", "attn"), None, "expert")),
        check_vma=False,
    )
```

```python
import functools

import jax
import jax.numpy as jnp
from jax import lax
from jax.experimental import pallas as pl
from jax.experimental.pallas import tpu as pltpu
from jax.sharding import PartitionSpec as P

D = 6144
HD = 128
PAGE = 16
CAP = 12
EPSILON = 1e-05
HALF = D // 2
QUARTER = D // 4
LO = 8
SLOT_COLS = HALF + QUARTER
LANES = 128
SCORE_SCALE = HD ** (-0.5)
NEG = -(2.0**100)
F32 = jnp.float32
BF16 = jnp.bfloat16
VMEM = pl.BlockSpec(memory_space=pltpu.VMEM)
SMEM = pl.BlockSpec(memory_space=pltpu.SMEM)
HBM = pl.BlockSpec(memory_space=pltpu.HBM)


def iota(shape, dim):
    return lax.broadcasted_iota(jnp.int32, shape, dim)


def eye(size):
    return iota((size, size), 0) == iota((size, size), 1)


def to_column(row, size):
    return jnp.sum(jnp.where(eye(size), row, 0.0), axis=1, keepdims=True)


def to_row(column, size):
    return jnp.sum(jnp.where(eye(size), column, 0.0), axis=0, keepdims=True)


def dot(a, b):
    return lax.dot_general(a, b, (((1,), (0,)), ((), ())), preferred_element_type=F32)


def dot_t(a, b):
    return lax.dot_general(a, b, (((1,), (1,)), ((), ())), preferred_element_type=F32)


def members(routes, expert):
    return jnp.max(jnp.where(routes == expert, 1.0, 0.0), axis=0, keepdims=True)


def mix_slots(shape, dim, part):
    index = iota(shape, dim)
    here = (index >= 4 * part) & (index < 4 * part + 4)
    return jnp.where(here, index - 4 * part + LO, -1).astype(F32)


def split_three(value):
    high = value.astype(BF16)
    rest = value - high.astype(F32)
    middle = rest.astype(BF16)
    low = (rest - middle.astype(F32)).astype(BF16)
    return high.astype(F32), middle.astype(F32), low.astype(F32)


def attend_kernel(hosted, *refs):
    sources, (hidden, kept, other), held_here, sems = refs[:11], refs[11:14], refs[14:25], refs[25]
    counts, tails, order, routes, mig_pages, mig_dest, queries, new_kv, residual, gain, pool = held_here
    rows = queries.shape[0]
    tokens = pool.shape[0]
    pages = tokens // PAGE
    heads_here = pool.shape[1] // (2 * HD)
    group = queries.shape[1] // (heads_here * HD)

    copies = [
        pltpu.make_async_copy(a, b, sems.at[k]) for k, (a, b) in enumerate(zip(sources[:-1], held_here[:-1]))
    ]
    for head in range(heads_here):
        columns = pl.ds(2 * head * HD, 2 * HD)
        copies.append(
            pltpu.make_async_copy(sources[-1].at[:, columns], pool.at[:, columns], sems.at[len(sources) - 1 + head])
        )
    for copy in copies[:8] + copies[10:] + copies[8:10]:
        copy.start()
    for copy in copies[:6]:
        copy.wait()

    counts_row = counts[...].astype(F32)
    row_a, row_b = iota((rows, rows), 0), iota((rows, rows), 1)
    first = jnp.sum(jnp.where(row_b < row_a, counts_row, 0.0), axis=1, keepdims=True)
    count = to_column(counts_row, rows)
    tail = to_column(tails[...].astype(F32), rows)
    place = iota((rows, pages), 1).astype(F32)
    inside = (place >= first) & (place < first + count)
    held = jnp.where(inside, jnp.where(place == first + count - 1.0, tail, float(PAGE)), 0.0)
    page_at = to_column(order[...].astype(F32), pages)
    page_of = (iota((pages, tokens), 1) // PAGE).astype(F32)
    placed = jnp.where(page_at == page_of, 1.0, 0.0).astype(BF16)
    limit = dot(held.astype(BF16), placed)
    visible = (iota((rows, tokens), 1) % PAGE).astype(F32) < limit
    copies[6].wait()
    copies[7].wait()
    squares = jnp.zeros((rows, HD), F32)
    penalty = jnp.where(visible, 0.0, NEG)[None]
    own_penalty = jnp.where(eye(rows), 0.0, NEG)[None]
    def qk(head):
        base = head * group * HD
        query = jnp.concatenate(
            [queries[:, base + g * HD : base + (g + 1) * HD] for g in range(group)], axis=0
        )
        keys = slice(2 * head * HD, (2 * head + 1) * HD)
        scores = dot_t(query, pool[:, keys])
        own = dot_t(query, new_kv[:, keys])
        scores = (scores.reshape(group, rows, tokens) + penalty).reshape(group * rows, tokens)
        own = (own.reshape(group, rows, rows) + own_penalty).reshape(group * rows, rows)
        return scores, own
    def soft(so):
        scores, own = so
        top = jnp.maximum(
            jnp.max(scores, axis=1, keepdims=True), jnp.max(own, axis=1, keepdims=True)
        )
        weights = jnp.exp((scores - top) * SCORE_SCALE)
        own_weights = jnp.exp((own - top) * SCORE_SCALE)
        total = jnp.sum(weights, axis=1, keepdims=True) + jnp.sum(own_weights, axis=1, keepdims=True)
        inverse = 1.0 / total
        return (weights * inverse).astype(BF16), (own_weights * inverse).astype(BF16)
    def pv(head, w, squares):
        base = head * group * HD
        values = slice((2 * head + 1) * HD, (2 * head + 2) * HD)
        mixed = dot(w[0], pool[:, values])
        mixed = mixed + dot(w[1], new_kv[:, values])
        for g in range(group):
            columns = slice(base + g * HD, base + (g + 1) * HD)
            part = residual[:, columns].astype(F32) + mixed[g * rows : (g + 1) * rows]
            hidden[:, columns] = part
            squares = squares + part * part
        return squares
    s = []
    for head in range(heads_here):
        if head % 2 == 0:
            copies[10 + head].wait()
            copies[11 + head].wait()
        s.append(qk(head))
    copies[8].wait()
    copies[9].wait()
    for head in range(heads_here):
        squares = pv(head, soft(s[head]), squares)
    square_row = to_row(jnp.sum(squares, axis=1, keepdims=True), rows)

    scaled = (hidden[...] * gain[...]).astype(BF16)
    lows, mixes = [], []
    for expert in range(hosted):
        member_row = members(routes[...], expert)
        member = to_column(member_row, rows)
        rank = jnp.sum(jnp.where(row_a <= row_b, member, 0.0), axis=0, keepdims=True) - 1.0
        rank = jnp.where(member_row > 0.0, rank, -2.0)
        lows.append(rank == iota((LO, rows), 0).astype(F32))
        mixes.append([rank == mix_slots((LO, rows), 0, part) for part in range(2)])
    picked = []
    for part in range(2):
        maps = [jnp.where(m, 1.0, 0.0) for m in lows] + [jnp.where(m[part], 1.0, 0.0) for m in mixes]
        stacked = jnp.concatenate(maps, axis=0).astype(BF16)
        picked.append(dot(stacked, scaled[:, part * QUARTER : (part + 1) * QUARTER]))
    lane = iota((LO, LANES), 1)
    by_expert = []
    for expert in range(hosted):
        low_at, mix_at = expert * LO, (hosted + expert) * LO
        low_sum = jnp.sum(jnp.where(lows[expert], square_row, 0.0), axis=1, keepdims=True)
        mix_map = mixes[expert][0] | mixes[expert][1]
        mix_sum = jnp.sum(jnp.where(mix_map, square_row, 0.0), axis=1, keepdims=True)
        extra = jnp.zeros((LO, LANES), F32)
        for at, piece in enumerate(split_three(low_sum) + split_three(mix_sum)):
            extra = jnp.where(lane == at, piece, extra)
        low_rows = [picked[part][low_at : low_at + LO] for part in range(2)]
        mixed_rows = picked[0][mix_at : mix_at + LO] + picked[1][mix_at : mix_at + LO]
        by_expert.append(jnp.concatenate(low_rows + [mixed_rows, extra], axis=1))
    first_half = lax.axis_index("expert") == 0
    extra_at = SLOT_COLS + LANES
    mine = jnp.where(first_half, by_expert[0], by_expert[1])
    kept[:, :extra_at] = jnp.concatenate([mine, jnp.zeros_like(mine)], axis=0).astype(BF16)
    other[...] = jnp.where(first_half, by_expert[1], by_expert[0]).astype(BF16)

    entries = mig_pages.shape[1]
    page_width = pool.shape[1]
    lane = iota((PAGE, LANES), 1)
    notes = jnp.where(lane == entries, lax.axis_index("attn").astype(F32), 0.0)
    for entry in range(entries):
        start = pl.multiple_of(mig_pages[0, entry] * PAGE, PAGE)
        at = extra_at + entry * page_width
        kept[:, at : at + page_width] = pool[pl.ds(start, PAGE), :]
        notes = jnp.where(lane == entry, mig_dest[0, entry].astype(F32), notes)
    kept[:, extra_at + entries * page_width :] = notes.astype(BF16)


def pack_kernel(kept, theirs, message):
    lane = iota((LO, LANES), 1)
    mine = kept[:, : SLOT_COLS + LANES].astype(F32)[:LO]
    extra = mine[:, SLOT_COLS:] + theirs[:, SLOT_COLS:].astype(F32)
    low_scale = lax.rsqrt(jnp.sum(jnp.where(lane < 3, extra, 0.0), axis=1, keepdims=True) / D + EPSILON)
    mix_sum = jnp.sum(jnp.where((lane >= 3) & (lane < 6), extra, 0.0), axis=1, keepdims=True)
    mix_scale = lax.rsqrt(mix_sum / D + EPSILON)
    first_half = lax.axis_index("expert") == 0
    for columns, scale in ((slice(0, HALF), low_scale), (slice(HALF, SLOT_COLS), mix_scale)):
        a = mine[:, columns] * scale
        b = theirs[:, columns].astype(F32) * scale
        both = jnp.concatenate([jnp.where(first_half, a, b), jnp.where(first_half, b, a)], axis=0)
        message[:, columns] = both.astype(BF16)
    message[:, SLOT_COLS:] = kept[:, SLOT_COLS + LANES :]


def fetch_kernel(source, out, sem):
    copy = pltpu.make_async_copy(source, out, sem)
    copy.start()
    copy.wait()


def ffn_kernel(n, cut, *refs):
    blocks, (gate, up, down) = refs[: n + 1], refs[n + 1 : n + 4]
    outs = refs[n + 4 : 2 * n + 4]
    low_rows, mix_rows, gate_sum, up_sum = refs[2 * n + 4 :]
    for j in range(n - 1):
        low_rows[16 * j : 16 * j + 16, :] = blocks[j][:, :HALF]
        mix_rows[16 * j : 16 * j + 16, :] = blocks[j][:, HALF:SLOT_COLS]
    j = n - 1
    low_rows[16 * j : 16 * j + 16, :] = blocks[j][:, :HALF]
    mix_rows[16 * j : 16 * j + 16, : cut - HALF] = blocks[j][:, HALF:cut]
    mix_rows[16 * j : 16 * j + 16, cut - HALF :] = blocks[n][:, : SLOT_COLS - cut]

    size = min(n, 8)
    span = 16 * size
    row = iota((span, 1), 0) % 16
    for q in range(4):
        low_here, mix_here = (row // 8) == q // 2, (row // 4) == q
        part = slice(q * QUARTER, (q + 1) * QUARTER)
        within = slice((q % 2) * QUARTER, (q % 2 + 1) * QUARTER)
        for at in range(0, 16 * n, span):
            left = jnp.concatenate([low_rows[at : at + span, within], mix_rows[at : at + span, :]], axis=0)
            for weight, total in ((gate, gate_sum), (up, up_sum)):
                product = dot(left, weight[part, :])
                low = jnp.where(low_here, product[:span], 0.0)
                mix = jnp.where(mix_here, product[span:], 0.0)
                if q == 0:
                    total[0, at : at + span, :] = low
                    total[1, at : at + span, :] = mix
                else:
                    total[0, at : at + span, :] += low
                    total[1, at : at + span, :] += mix

    lower = iota((8 * size, 1), 0) % 8 < 4
    width = gate.shape[1]

    def fold(total, at):
        low, mix = [
            jnp.sum(total[k, at : at + span, :].reshape(size, 2, 8, width), axis=1).reshape(8 * size, width)
            for k in range(2)
        ]
        other = jnp.where(lower, pltpu.roll(mix, 8 * size - 4, 0), pltpu.roll(mix, 4, 0))
        return low, mix + other

    first_rows = iota((8, 1), 0) < 4
    for at in range(0, 16 * n, span):
        pieces = [jax.nn.silu(g) * u for g, u in zip(fold(gate_sum, at), fold(up_sum, at))]
        active = jnp.concatenate([p.reshape(size, 8, width) for p in pieces], axis=1)
        active = active.reshape(span, width).astype(BF16)
        quarters = [dot(active, down[:, q * QUARTER : (q + 1) * QUARTER]) for q in range(4)]
        for j in range(size):
            out = outs[at // 16 + j]
            low_at, mix_at = slice(16 * j, 16 * j + 8), slice(16 * j + 8, 16 * j + 16)
            for part in range(2):
                both = jnp.concatenate([quarters[part][low_at], quarters[2 + part][low_at]], axis=0)
                out[:, part * QUARTER : (part + 1) * QUARTER] = both.astype(BF16)
            both = jnp.concatenate(
                [jnp.where(first_rows, quarters[k][mix_at], quarters[k + 1][mix_at]) for k in (0, 2)], axis=0
            )
            out[:, HALF:] = both.astype(BF16)


def arrive_kernel(n, cut, page_width, *refs):
    blocks, (arrived, board, board_smem, sem) = refs[: n + 1], refs[n + 1 :]
    entries = arrived.shape[0]
    notes_at = SLOT_COLS + entries * page_width
    heads = [block[:, notes_at:].astype(F32)[0:1] for block in blocks[: n - 1]]
    heads.append(blocks[n][:, notes_at - cut :].astype(F32)[0:1])
    notes = jnp.concatenate(heads, axis=0)
    lane = iota((n, LANES), 1)
    match = (notes == lax.axis_index("attn").astype(F32)) & (lane < entries)
    named = jnp.max(jnp.where(match, 1.0, 0.0), axis=1, keepdims=True)
    source = jnp.sum(jnp.where(lane == entries, notes, 0.0), axis=1, keepdims=True)
    earlier = to_row(source, n) < source
    rank = jnp.sum(jnp.where(earlier, to_row(named, n), 0.0), axis=1, keepdims=True)
    board[...] = jnp.where(match, rank, -1.0).astype(jnp.int32)
    copy = pltpu.make_async_copy(board, board_smem, sem)
    copy.start()
    arrived[...] = jnp.zeros_like(arrived)
    copy.wait()
    for j in range(n):
        block, shift = (blocks[j], 0) if j < n - 1 else (blocks[n], cut)
        for entry in range(entries):
            slot = board_smem[j, entry]
            at = SLOT_COLS + entry * page_width - shift

            @pl.when((slot >= 0) & (slot < entries))
            def _():
                arrived[slot] = block[:, at : at + page_width]


def finish_kernel(own, from_left, from_right, mine, other):
    total = own[...].astype(F32) + from_left[...].astype(F32) + from_right[...].astype(F32)
    first_half = lax.axis_index("expert") == 0
    top, bottom = total[:LO], total[LO:]
    mine[...] = jnp.where(first_half, top, bottom).astype(BF16)
    other[...] = jnp.where(first_half, bottom, top).astype(BF16)


def combine_kernel(hosted, hidden, mine, theirs, routes, gates, layer_out):
    rows = hidden.shape[0]
    first_half = lax.axis_index("expert") == 0
    a, b = mine[...].astype(F32), theirs[...].astype(F32)
    by_expert = [jnp.where(first_half, a, b).astype(BF16), jnp.where(first_half, b, a).astype(BF16)]
    row_a, row_b = iota((rows, rows), 0), iota((rows, rows), 1)
    terms = [[], []]
    for expert in range(hosted):
        member = members(routes[...], expert)
        share = jnp.sum(jnp.where(routes[...] == expert, gates[...], 0.0), axis=0, keepdims=True)
        share = to_column(share, rows)
        rank = jnp.sum(jnp.where(row_b <= row_a, member, 0.0), axis=1, keepdims=True) - 1.0
        rank = jnp.where(to_column(member, rows) > 0.0, rank, -2.0)
        low = jnp.where(rank == iota((rows, LO), 1).astype(F32), 1.0, 0.0).astype(BF16)
        for part in range(2):
            columns = slice(part * QUARTER, (part + 1) * QUARTER)
            mix = jnp.where(rank == mix_slots((rows, LO), 1, part), 1.0, 0.0).astype(BF16)
            value = dot(low, by_expert[expert][:, columns]) + dot(mix, by_expert[expert][:, HALF:])
            terms[part].append(share * value)
    for part in range(2):
        columns = slice(part * QUARTER, (part + 1) * QUARTER)
        layer_out[:, columns] = (hidden[:, columns] + (terms[part][0] + terms[part][1])).astype(BF16)


def call(kernel, outs, in_specs, args, scratch=(), flops=0, bytes_accessed=0, vmem=16 << 20):
    many = isinstance(outs, (list, tuple))
    return pl.pallas_call(
        kernel,
        out_shape=outs,
        in_specs=in_specs,
        out_specs=[VMEM] * len(outs) if many else VMEM,
        scratch_shapes=list(scratch),
        compiler_params=pltpu.CompilerParams(vmem_limit_bytes=vmem),
        cost_estimate=pl.CostEstimate(flops=flops, bytes_accessed=bytes_accessed, transcendentals=0),
    )(*args)


def ring_order(n):
    return [0, 2, 4, 6, 7, 5, 3, 1] if n == 8 else list(range(n))


def fetch_weight(shape, weight):
    return call(
        fetch_kernel,
        shape(weight.shape, BF16),
        [HBM],
        (weight,),
        scratch=(pltpu.SemaphoreType.DMA,),
        bytes_accessed=6_400_000,
    )


def add(a, b):
    return (a.astype(F32) + b.astype(F32)).astype(BF16)


def per_device(
    n,
    hosted,
    queries,
    new_kv,
    kv_pool,
    page_counts,
    tail_tokens,
    page_order,
    residual,
    norm_gain,
    routes,
    route_gates,
    w_gate,
    w_up,
    w_down,
    mig_pages,
    mig_dest,
):
    rows, width = queries.shape
    page_width = kv_pool.shape[2]
    entries = mig_pages.shape[1]
    pool = kv_pool.reshape(-1, page_width)
    around = ring_order(n)
    right = [(around[i], around[(i + 1) % n]) for i in range(n)]
    left = [(b, a) for a, b in right]
    swap = [(0, 1), (1, 0)]
    shape = jax.ShapeDtypeStruct

    moved_cols = entries * page_width + LANES
    sources = (
        page_counts,
        tail_tokens.reshape(1, -1),
        page_order,
        routes.T,
        mig_pages,
        mig_dest,
        queries,
        new_kv,
        residual,
        norm_gain.reshape(1, -1),
        pool,
    )
    spaces = [pltpu.VMEM] * 4 + [pltpu.SMEM] * 2 + [pltpu.VMEM] * 5
    hidden, kept, other = call(
        functools.partial(attend_kernel, hosted),
        [
            shape((rows, width), F32),
            shape((2 * LO, SLOT_COLS + LANES + moved_cols), BF16),
            shape((LO, SLOT_COLS + LANES), BF16),
        ],
        [HBM] * len(sources),
        sources,
        scratch=[space(x.shape, x.dtype) for space, x in zip(spaces, sources)]
        + [pltpu.SemaphoreType.DMA((len(sources) + page_width // (2 * HD),))],
        flops=500_000_000,
        bytes_accessed=3_500_000,
        vmem=60 << 20,
    )
    theirs = lax.ppermute(other, "expert", swap)
    message = call(
        pack_kernel,
        shape((2 * LO, SLOT_COLS + moved_cols), BF16),
        [VMEM] * 2,
        (kept, theirs),
        flops=500_000,
        bytes_accessed=500_000,
    )

    far = n // 2
    cut = HALF + 3 * LANES
    tie = lax.optimization_barrier
    fetch = functools.partial(fetch_weight, shape)
    from_left, from_right = [message], [message]
    weights, stored = [], [w_gate[0], w_up[0], w_down[0]]
    for step in range(far):
        a, b = from_left[-1], from_right[-1]
        if step == far - 1:
            a, b = a[:, :cut], b[:, cut:]
        a, b = lax.ppermute(a, "attn", right), lax.ppermute(b, "attn", left)
        if step < len(stored):
            weights.append(fetch(stored[step]))
            a, weights[-1] = tie((a, weights[-1]))
        from_left.append(a)
        from_right.append(b)
    last_a, last_b = from_left.pop(), from_right.pop()
    blocks = [message] + from_left[1:] + from_right[1:] + [last_a, last_b]

    ff = w_gate.shape[2]
    size = 16 * n
    outs = call(
        functools.partial(ffn_kernel, n, cut),
        [shape((2 * LO, SLOT_COLS), BF16)] * n,
        [VMEM] * (n + 4),
        (*blocks, *weights),
        scratch=(
            pltpu.VMEM((size, HALF), BF16),
            pltpu.VMEM((size, QUARTER), BF16),
            pltpu.VMEM((2, size, ff), F32),
            pltpu.VMEM((2, size, ff), F32),
        ),
        flops=2_000_000_000,
        bytes_accessed=12_000_000,
    )

    to_left = {k: outs[k] for k in range(1, far)}
    to_right = {k: outs[far - 1 + k] for k in range(1, far)}
    split = SLOT_COLS // 2
    going_right = lax.ppermute(outs[n - 1][:, :split], "attn", right)
    going_left = lax.ppermute(outs[n - 1][:, split:], "attn", left)
    arrived = call(
        functools.partial(arrive_kernel, n, cut, page_width),
        shape((entries, PAGE, page_width), BF16),
        [VMEM] * (n + 1),
        tuple(blocks),
        scratch=(
            pltpu.VMEM((n, LANES), jnp.int32),
            pltpu.SMEM((n, LANES), jnp.int32),
            pltpu.SemaphoreType.DMA,
        ),
        flops=100_000,
        bytes_accessed=2_000_000,
    )
    going_right, arrived = tie((going_right, arrived))
    for k in range(far - 1, 0, -1):
        if k == far - 1:
            send_right = jnp.concatenate([add(to_right[k][:, :split], going_right), to_right[k][:, split:]], axis=1)
            send_left = jnp.concatenate([to_left[k][:, :split], add(to_left[k][:, split:], going_left)], axis=1)
        else:
            send_right, send_left = add(to_right[k], going_right), add(to_left[k], going_left)
        going_right = lax.ppermute(send_right, "attn", right)
        going_left = lax.ppermute(send_left, "attn", left)
    kept, other_half = call(
        finish_kernel,
        [shape((LO, SLOT_COLS), BF16)] * 2,
        [VMEM] * 3,
        (outs[0], going_right, going_left),
        flops=500_000,
        bytes_accessed=600_000,
    )
    returned = lax.ppermute(other_half, "expert", swap)
    layer_out = call(
        functools.partial(combine_kernel, hosted),
        shape((rows, width), BF16),
        [VMEM] * 5,
        (hidden, kept, returned, routes.T, route_gates.T),
        flops=20_000_000,
        bytes_accessed=800_000,
    )
    return layer_out, arrived


def solution(mesh):
    n, hosted = mesh.shape["attn"], mesh.shape["expert"]
    return jax.shard_map(
        functools.partial(per_device, n, hosted),
        mesh=mesh,
        in_specs=(
            P(("groups", "attn"), "expert"),
            P(("groups", "attn"), "expert"),
            P(("groups", "attn"), None, "expert"),
            P(("groups", "attn"), None),
            P(("groups", "attn")),
            P(("groups", "attn"), None),
            P(("groups", "attn"), "expert"),
            P("expert"),
            P(("groups", "attn"), None),
            P(("groups", "attn"), None),
            P("expert", None, "attn"),
            P("expert", None, "attn"),
            P("expert", "attn", None),
            P(("groups", "attn"), None),
            P(("groups", "attn"), None),
        ),
        out_specs=(P(("groups", "attn"), "expert"), P(("groups", "attn"), None, "expert")),
        check_vma=False,
    )
```

```python
import functools

import jax
import jax.numpy as jnp
from jax import lax
from jax.experimental import pallas as pl
from jax.experimental.pallas import tpu as pltpu
from jax.sharding import PartitionSpec as P

D = 6144
HD = 128
PAGE = 16
CAP = 12
EPSILON = 1e-05
HALF = D // 2
QUARTER = D // 4
LO = 8
SLOT_COLS = HALF + QUARTER
LANES = 128
SCORE_SCALE = HD ** (-0.5)
NEG = -(2.0**100)
F32 = jnp.float32
BF16 = jnp.bfloat16
VMEM = pl.BlockSpec(memory_space=pltpu.VMEM)
SMEM = pl.BlockSpec(memory_space=pltpu.SMEM)
HBM = pl.BlockSpec(memory_space=pltpu.HBM)


def iota(shape, dim):
    return lax.broadcasted_iota(jnp.int32, shape, dim)


def eye(size):
    return iota((size, size), 0) == iota((size, size), 1)


def to_column(row, size):
    return jnp.sum(jnp.where(eye(size), row, 0.0), axis=1, keepdims=True)


def to_row(column, size):
    return jnp.sum(jnp.where(eye(size), column, 0.0), axis=0, keepdims=True)


def dot(a, b):
    return lax.dot_general(a, b, (((1,), (0,)), ((), ())), preferred_element_type=F32)


def dot_t(a, b):
    return lax.dot_general(a, b, (((1,), (1,)), ((), ())), preferred_element_type=F32)


def members(routes, expert):
    return jnp.max(jnp.where(routes == expert, 1.0, 0.0), axis=0, keepdims=True)


def mix_slots(shape, dim, part):
    index = iota(shape, dim)
    here = (index >= 4 * part) & (index < 4 * part + 4)
    return jnp.where(here, index - 4 * part + LO, -1).astype(F32)


def split_three(value):
    high = value.astype(BF16)
    rest = value - high.astype(F32)
    middle = rest.astype(BF16)
    low = (rest - middle.astype(F32)).astype(BF16)
    return high.astype(F32), middle.astype(F32), low.astype(F32)


def attend_kernel(hosted, *refs):
    sources, (hidden, kept, other), held_here, sems = refs[:11], refs[11:14], refs[14:25], refs[25]
    counts, tails, order, routes, mig_pages, mig_dest, queries, new_kv, residual, gain, pool = held_here
    rows = queries.shape[0]
    tokens = pool.shape[0]
    pages = tokens // PAGE
    heads_here = pool.shape[1] // (2 * HD)
    group = queries.shape[1] // (heads_here * HD)

    copies = [
        pltpu.make_async_copy(a, b, sems.at[k]) for k, (a, b) in enumerate(zip(sources[:-1], held_here[:-1]))
    ]
    for head in range(heads_here):
        columns = pl.ds(2 * head * HD, 2 * HD)
        copies.append(
            pltpu.make_async_copy(sources[-1].at[:, columns], pool.at[:, columns], sems.at[len(sources) - 1 + head])
        )
    for copy in copies[:8] + copies[10:] + copies[8:10]:
        copy.start()
    for copy in copies[:6]:
        copy.wait()

    counts_row = counts[...].astype(F32)
    row_a, row_b = iota((rows, rows), 0), iota((rows, rows), 1)
    first = jnp.sum(jnp.where(row_b < row_a, counts_row, 0.0), axis=1, keepdims=True)
    count = to_column(counts_row, rows)
    tail = to_column(tails[...].astype(F32), rows)
    place = iota((rows, pages), 1).astype(F32)
    inside = (place >= first) & (place < first + count)
    held = jnp.where(inside, jnp.where(place == first + count - 1.0, tail, float(PAGE)), 0.0)
    page_at = to_column(order[...].astype(F32), pages)
    page_of = (iota((pages, tokens), 1) // PAGE).astype(F32)
    placed = jnp.where(page_at == page_of, 1.0, 0.0).astype(BF16)
    limit = dot(held.astype(BF16), placed)
    visible = (iota((rows, tokens), 1) % PAGE).astype(F32) < limit
    copies[6].wait()
    copies[7].wait()
    squares = jnp.zeros((rows, HD), F32)
    penalty = jnp.where(visible, 0.0, NEG)[None]
    own_penalty = jnp.where(eye(rows), 0.0, NEG)[None]
    def qk(head):
        base = head * group * HD
        query = jnp.concatenate(
            [queries[:, base + g * HD : base + (g + 1) * HD] for g in range(group)], axis=0
        )
        keys = slice(2 * head * HD, (2 * head + 1) * HD)
        scores = dot_t(query, pool[:, keys])
        own = dot_t(query, new_kv[:, keys])
        scores = (scores.reshape(group, rows, tokens) + penalty).reshape(group * rows, tokens)
        own = (own.reshape(group, rows, rows) + own_penalty).reshape(group * rows, rows)
        return scores, own
    def soft(so):
        scores, own = so
        top = jnp.maximum(
            jnp.max(scores, axis=1, keepdims=True), jnp.max(own, axis=1, keepdims=True)
        )
        weights = jnp.exp((scores - top) * SCORE_SCALE)
        own_weights = jnp.exp((own - top) * SCORE_SCALE)
        total = jnp.sum(weights, axis=1, keepdims=True) + jnp.sum(own_weights, axis=1, keepdims=True)
        inverse = 1.0 / total
        return (weights * inverse).astype(BF16), (own_weights * inverse).astype(BF16)
    def pv(head, w, squares):
        base = head * group * HD
        values = slice((2 * head + 1) * HD, (2 * head + 2) * HD)
        mixed = dot(w[0], pool[:, values])
        mixed = mixed + dot(w[1], new_kv[:, values])
        for g in range(group):
            columns = slice(base + g * HD, base + (g + 1) * HD)
            part = residual[:, columns].astype(F32) + mixed[g * rows : (g + 1) * rows]
            hidden[:, columns] = part
            squares = squares + part * part
        return squares
    s = []
    for head in range(heads_here):
        if head % 2 == 0:
            copies[10 + head].wait()
            copies[11 + head].wait()
        s.append(qk(head))
    copies[8].wait()
    copies[9].wait()
    for head in range(heads_here):
        squares = pv(head, soft(s[head]), squares)
    square_row = to_row(jnp.sum(squares, axis=1, keepdims=True), rows)

    scaled = (hidden[...] * gain[...]).astype(BF16)
    lows, mixes = [], []
    for expert in range(hosted):
        member_row = members(routes[...], expert)
        member = to_column(member_row, rows)
        rank = jnp.sum(jnp.where(row_a <= row_b, member, 0.0), axis=0, keepdims=True) - 1.0
        rank = jnp.where(member_row > 0.0, rank, -2.0)
        lows.append(rank == iota((LO, rows), 0).astype(F32))
        mixes.append([rank == mix_slots((LO, rows), 0, part) for part in range(2)])
    picked = []
    for part in range(2):
        maps = [jnp.where(m, 1.0, 0.0) for m in lows] + [jnp.where(m[part], 1.0, 0.0) for m in mixes]
        stacked = jnp.concatenate(maps, axis=0).astype(BF16)
        picked.append(dot(stacked, scaled[:, part * QUARTER : (part + 1) * QUARTER]))
    lane = iota((LO, LANES), 1)
    by_expert = []
    for expert in range(hosted):
        low_at, mix_at = expert * LO, (hosted + expert) * LO
        low_sum = jnp.sum(jnp.where(lows[expert], square_row, 0.0), axis=1, keepdims=True)
        mix_map = mixes[expert][0] | mixes[expert][1]
        mix_sum = jnp.sum(jnp.where(mix_map, square_row, 0.0), axis=1, keepdims=True)
        extra = jnp.zeros((LO, LANES), F32)
        for at, piece in enumerate(split_three(low_sum) + split_three(mix_sum)):
            extra = jnp.where(lane == at, piece, extra)
        low_rows = [picked[part][low_at : low_at + LO] for part in range(2)]
        mixed_rows = picked[0][mix_at : mix_at + LO] + picked[1][mix_at : mix_at + LO]
        by_expert.append(jnp.concatenate(low_rows + [mixed_rows, extra], axis=1))
    first_half = lax.axis_index("expert") == 0
    extra_at = SLOT_COLS + LANES
    mine = jnp.where(first_half, by_expert[0], by_expert[1])
    kept[:, :extra_at] = jnp.concatenate([mine, jnp.zeros_like(mine)], axis=0).astype(BF16)
    other[...] = jnp.where(first_half, by_expert[1], by_expert[0]).astype(BF16)

    entries = mig_pages.shape[1]
    page_width = pool.shape[1]
    lane = iota((PAGE, LANES), 1)
    notes = jnp.where(lane == entries, lax.axis_index("attn").astype(F32), 0.0)
    for entry in range(entries):
        start = pl.multiple_of(mig_pages[0, entry] * PAGE, PAGE)
        at = extra_at + entry * page_width
        kept[:, at : at + page_width] = pool[pl.ds(start, PAGE), :]
        notes = jnp.where(lane == entry, mig_dest[0, entry].astype(F32), notes)
    kept[:, extra_at + entries * page_width :] = notes.astype(BF16)


def pack_kernel(kept, theirs, message):
    lane = iota((LO, LANES), 1)
    mine = kept[:, : SLOT_COLS + LANES].astype(F32)[:LO]
    extra = mine[:, SLOT_COLS:] + theirs[:, SLOT_COLS:].astype(F32)
    low_scale = lax.rsqrt(jnp.sum(jnp.where(lane < 3, extra, 0.0), axis=1, keepdims=True) / D + EPSILON)
    mix_sum = jnp.sum(jnp.where((lane >= 3) & (lane < 6), extra, 0.0), axis=1, keepdims=True)
    mix_scale = lax.rsqrt(mix_sum / D + EPSILON)
    first_half = lax.axis_index("expert") == 0
    for columns, scale in ((slice(0, HALF), low_scale), (slice(HALF, SLOT_COLS), mix_scale)):
        a = mine[:, columns] * scale
        b = theirs[:, columns].astype(F32) * scale
        both = jnp.concatenate([jnp.where(first_half, a, b), jnp.where(first_half, b, a)], axis=0)
        message[:, columns] = both.astype(BF16)
    message[:, SLOT_COLS:] = kept[:, SLOT_COLS + LANES :]


def copy_kernel(source, out):
    out[...] = source[...]


def fetch_kernel(source, out, sem):
    copy = pltpu.make_async_copy(source, out, sem)
    copy.start()
    copy.wait()


def ffn_kernel(cut, *refs):
    count = len(refs) // 2 - 3 if cut is None else 1
    pieces = count if cut is None else 2
    blocks, (gate, up, down) = refs[:pieces], refs[pieces : pieces + 3]
    outs = refs[pieces + 3 : pieces + 3 + count]
    low_rows, mix_rows, gate_sum, up_sum = refs[pieces + 3 + count :]
    if cut is None:
        for j in range(count):
            low_rows[16 * j : 16 * j + 16, :] = blocks[j][:, :HALF]
            mix_rows[16 * j : 16 * j + 16, :] = blocks[j][:, HALF:SLOT_COLS]
    else:
        low_rows[...] = blocks[0][:, :HALF]
        mix_rows[:, : cut - HALF] = blocks[0][:, HALF:cut]
        mix_rows[:, cut - HALF :] = blocks[1][:, : SLOT_COLS - cut]

    groups = [(first, min(8, count - first)) for first in range(0, count, 8)]
    width = gate.shape[1]
    for q in range(4):
        part = slice(q * QUARTER, (q + 1) * QUARTER)
        within = slice((q % 2) * QUARTER, (q % 2 + 1) * QUARTER)
        for first, size in groups:
            at, span = 16 * first, 16 * size
            row = iota((span, 1), 0) % 16
            low_here, mix_here = (row // 8) == q // 2, (row // 4) == q
            left = jnp.concatenate([low_rows[at : at + span, within], mix_rows[at : at + span, :]], axis=0)
            for weight, total in ((gate, gate_sum), (up, up_sum)):
                product = dot(left, weight[part, :])
                low = jnp.where(low_here, product[:span], 0.0)
                mix = jnp.where(mix_here, product[span:], 0.0)
                if q == 0:
                    total[0, at : at + span, :] = low
                    total[1, at : at + span, :] = mix
                else:
                    total[0, at : at + span, :] += low
                    total[1, at : at + span, :] += mix

    def fold(total, at, size):
        low, mix = [
            jnp.sum(total[k, at : at + 16 * size, :].reshape(size, 2, 8, width), axis=1).reshape(8 * size, width)
            for k in range(2)
        ]
        lower = iota((8 * size, 1), 0) % 8 < 4
        other = jnp.where(lower, pltpu.roll(mix, 8 * size - 4, 0), pltpu.roll(mix, 4, 0))
        return low, mix + other

    first_rows = iota((8, 1), 0) < 4
    for first, size in groups:
        at = 16 * first
        pieces = [jax.nn.silu(g) * u for g, u in zip(fold(gate_sum, at, size), fold(up_sum, at, size))]
        active = jnp.concatenate([p.reshape(size, 8, width) for p in pieces], axis=1)
        active = active.reshape(16 * size, width).astype(BF16)
        quarters = [dot(active, down[:, q * QUARTER : (q + 1) * QUARTER]) for q in range(4)]
        for j in range(size):
            out = outs[first + j]
            low_at, mix_at = slice(16 * j, 16 * j + 8), slice(16 * j + 8, 16 * j + 16)
            for part in range(2):
                both = jnp.concatenate([quarters[part][low_at], quarters[2 + part][low_at]], axis=0)
                out[:, part * QUARTER : (part + 1) * QUARTER] = both.astype(BF16)
            both = jnp.concatenate(
                [jnp.where(first_rows, quarters[k][mix_at], quarters[k + 1][mix_at]) for k in (0, 2)], axis=0
            )
            out[:, HALF:] = both.astype(BF16)


def arrive_kernel(n, cut, page_width, *refs):
    blocks, (arrived, board, board_smem, sem) = refs[: n + 1], refs[n + 1 :]
    entries = arrived.shape[0]
    notes_at = SLOT_COLS + entries * page_width
    heads = [block[:, notes_at:].astype(F32)[0:1] for block in blocks[: n - 1]]
    heads.append(blocks[n][:, notes_at - cut :].astype(F32)[0:1])
    notes = jnp.concatenate(heads, axis=0)
    lane = iota((n, LANES), 1)
    match = (notes == lax.axis_index("attn").astype(F32)) & (lane < entries)
    named = jnp.max(jnp.where(match, 1.0, 0.0), axis=1, keepdims=True)
    source = jnp.sum(jnp.where(lane == entries, notes, 0.0), axis=1, keepdims=True)
    earlier = to_row(source, n) < source
    rank = jnp.sum(jnp.where(earlier, to_row(named, n), 0.0), axis=1, keepdims=True)
    board[...] = jnp.where(match, rank, -1.0).astype(jnp.int32)
    copy = pltpu.make_async_copy(board, board_smem, sem)
    copy.start()
    arrived[...] = jnp.zeros_like(arrived)
    copy.wait()
    for j in range(n):
        block, shift = (blocks[j], 0) if j < n - 1 else (blocks[n], cut)
        for entry in range(entries):
            slot = board_smem[j, entry]
            at = SLOT_COLS + entry * page_width - shift

            @pl.when((slot >= 0) & (slot < entries))
            def _():
                arrived[slot] = block[:, at : at + page_width]


def finish_kernel(own, from_left, from_right, mine, other):
    total = own[...].astype(F32) + from_left[...].astype(F32) + from_right[...].astype(F32)
    first_half = lax.axis_index("expert") == 0
    top, bottom = total[:LO], total[LO:]
    mine[...] = jnp.where(first_half, top, bottom).astype(BF16)
    other[...] = jnp.where(first_half, bottom, top).astype(BF16)


def combine_kernel(hosted, hidden, mine, theirs, routes, gates, layer_out):
    rows = hidden.shape[0]
    first_half = lax.axis_index("expert") == 0
    a, b = mine[...].astype(F32), theirs[...].astype(F32)
    by_expert = [jnp.where(first_half, a, b).astype(BF16), jnp.where(first_half, b, a).astype(BF16)]
    row_a, row_b = iota((rows, rows), 0), iota((rows, rows), 1)
    terms = [[], []]
    for expert in range(hosted):
        member = members(routes[...], expert)
        share = jnp.sum(jnp.where(routes[...] == expert, gates[...], 0.0), axis=0, keepdims=True)
        share = to_column(share, rows)
        rank = jnp.sum(jnp.where(row_b <= row_a, member, 0.0), axis=1, keepdims=True) - 1.0
        rank = jnp.where(to_column(member, rows) > 0.0, rank, -2.0)
        low = jnp.where(rank == iota((rows, LO), 1).astype(F32), 1.0, 0.0).astype(BF16)
        for part in range(2):
            columns = slice(part * QUARTER, (part + 1) * QUARTER)
            mix = jnp.where(rank == mix_slots((rows, LO), 1, part), 1.0, 0.0).astype(BF16)
            value = dot(low, by_expert[expert][:, columns]) + dot(mix, by_expert[expert][:, HALF:])
            terms[part].append(share * value)
    for part in range(2):
        columns = slice(part * QUARTER, (part + 1) * QUARTER)
        layer_out[:, columns] = (hidden[:, columns] + (terms[part][0] + terms[part][1])).astype(BF16)


def call(kernel, outs, in_specs, args, scratch=(), flops=0, bytes_accessed=0, vmem=16 << 20):
    many = isinstance(outs, (list, tuple))
    return pl.pallas_call(
        kernel,
        out_shape=outs,
        in_specs=in_specs,
        out_specs=[VMEM] * len(outs) if many else VMEM,
        scratch_shapes=list(scratch),
        compiler_params=pltpu.CompilerParams(vmem_limit_bytes=vmem),
        cost_estimate=pl.CostEstimate(flops=flops, bytes_accessed=bytes_accessed, transcendentals=0),
    )(*args)


def ring_order(n):
    return [0, 2, 4, 6, 7, 5, 3, 1] if n == 8 else list(range(n))


def fetch_weight(shape, weight):
    return call(
        fetch_kernel,
        shape(weight.shape, BF16),
        [HBM],
        (weight,),
        scratch=(pltpu.SemaphoreType.DMA,),
        bytes_accessed=6_400_000,
    )


def add(a, b):
    return (a.astype(F32) + b.astype(F32)).astype(BF16)


def per_device(
    n,
    hosted,
    queries,
    new_kv,
    kv_pool,
    page_counts,
    tail_tokens,
    page_order,
    residual,
    norm_gain,
    routes,
    route_gates,
    w_gate,
    w_up,
    w_down,
    mig_pages,
    mig_dest,
):
    rows, width = queries.shape
    page_width = kv_pool.shape[2]
    entries = mig_pages.shape[1]
    pool = kv_pool.reshape(-1, page_width)
    around = ring_order(n)
    right = [(around[i], around[(i + 1) % n]) for i in range(n)]
    left = [(b, a) for a, b in right]
    swap = [(0, 1), (1, 0)]
    shape = jax.ShapeDtypeStruct

    moved_cols = entries * page_width + LANES
    sources = (
        page_counts,
        tail_tokens.reshape(1, -1),
        page_order,
        routes.T,
        mig_pages,
        mig_dest,
        queries,
        new_kv,
        residual,
        norm_gain.reshape(1, -1),
        pool,
    )
    spaces = [pltpu.VMEM] * 4 + [pltpu.SMEM] * 2 + [pltpu.VMEM] * 5
    hidden, kept, other = call(
        functools.partial(attend_kernel, hosted),
        [
            shape((rows, width), F32),
            shape((2 * LO, SLOT_COLS + LANES + moved_cols), BF16),
            shape((LO, SLOT_COLS + LANES), BF16),
        ],
        [HBM] * len(sources),
        sources,
        scratch=[space(x.shape, x.dtype) for space, x in zip(spaces, sources)]
        + [pltpu.SemaphoreType.DMA((len(sources) + page_width // (2 * HD),))],
        flops=500_000_000,
        bytes_accessed=3_500_000,
        vmem=60 << 20,
    )
    tie = lax.optimization_barrier
    theirs = lax.ppermute(other, "expert", swap)
    kept = call(copy_kernel, shape(kept.shape, BF16), [VMEM], (kept,), bytes_accessed=3_000_000)
    theirs, kept = tie((theirs, kept))
    message = call(
        pack_kernel,
        shape((2 * LO, SLOT_COLS + moved_cols), BF16),
        [VMEM] * 2,
        (kept, theirs),
        flops=500_000,
        bytes_accessed=500_000,
    )

    far = n // 2
    cut = HALF + 3 * LANES
    fetch = functools.partial(fetch_weight, shape)
    from_left, from_right = [message], [message]
    weights, stored = [], [w_gate[0], w_up[0], w_down[0]]
    for step in range(far):
        a, b = from_left[-1], from_right[-1]
        if step == far - 1:
            a, b = a[:, :cut], b[:, cut:]
        a, b = lax.ppermute(a, "attn", right), lax.ppermute(b, "attn", left)
        if step < len(stored):
            weights.append(fetch(stored[step]))
            a, weights[-1] = tie((a, weights[-1]))
        from_left.append(a)
        from_right.append(b)
    last_a, last_b = from_left.pop(), from_right.pop()
    blocks = [message] + from_left[1:] + from_right[1:]
    ff = w_gate.shape[2]

    def feed_forward(pieces, count, cut):
        return call(
            functools.partial(ffn_kernel, cut),
            [shape((2 * LO, SLOT_COLS), BF16)] * count,
            [VMEM] * (len(pieces) + 3),
            (*pieces, *weights),
            scratch=(
                pltpu.VMEM((16 * count, HALF), BF16),
                pltpu.VMEM((16 * count, QUARTER), BF16),
                pltpu.VMEM((2, 16 * count, ff), F32),
                pltpu.VMEM((2, 16 * count, ff), F32),
            ),
            flops=2_000_000_000,
            bytes_accessed=8_000_000,
        )

    outs = list(feed_forward(blocks, n - 1, None))
    last_a, outs[0] = tie((last_a, outs[0]))
    outs = outs + list(feed_forward((last_a, last_b), 1, cut))

    to_left = {k: outs[k] for k in range(1, far)}
    to_right = {k: outs[far - 1 + k] for k in range(1, far)}
    split = SLOT_COLS // 2
    going_right = lax.ppermute(outs[n - 1][:, :split], "attn", right)
    going_left = lax.ppermute(outs[n - 1][:, split:], "attn", left)
    arrived = call(
        functools.partial(arrive_kernel, n, cut, page_width),
        shape((entries, PAGE, page_width), BF16),
        [VMEM] * (n + 1),
        (*blocks, last_a, last_b),
        scratch=(
            pltpu.VMEM((n, LANES), jnp.int32),
            pltpu.SMEM((n, LANES), jnp.int32),
            pltpu.SemaphoreType.DMA,
        ),
        flops=100_000,
        bytes_accessed=2_000_000,
    )
    going_right, arrived = tie((going_right, arrived))
    for k in range(far - 1, 0, -1):
        if k == far - 1:
            send_right = jnp.concatenate([add(to_right[k][:, :split], going_right), to_right[k][:, split:]], axis=1)
            send_left = jnp.concatenate([to_left[k][:, :split], add(to_left[k][:, split:], going_left)], axis=1)
        else:
            send_right, send_left = add(to_right[k], going_right), add(to_left[k], going_left)
        going_right = lax.ppermute(send_right, "attn", right)
        going_left = lax.ppermute(send_left, "attn", left)
    kept, other_half = call(
        finish_kernel,
        [shape((LO, SLOT_COLS), BF16)] * 2,
        [VMEM] * 3,
        (outs[0], going_right, going_left),
        flops=500_000,
        bytes_accessed=600_000,
    )
    returned = lax.ppermute(other_half, "expert", swap)
    layer_out = call(
        functools.partial(combine_kernel, hosted),
        shape((rows, width), BF16),
        [VMEM] * 5,
        (hidden, kept, returned, routes.T, route_gates.T),
        flops=20_000_000,
        bytes_accessed=800_000,
    )
    return layer_out, arrived


def solution(mesh):
    n, hosted = mesh.shape["attn"], mesh.shape["expert"]
    return jax.shard_map(
        functools.partial(per_device, n, hosted),
        mesh=mesh,
        in_specs=(
            P(("groups", "attn"), "expert"),
            P(("groups", "attn"), "expert"),
            P(("groups", "attn"), None, "expert"),
            P(("groups", "attn"), None),
            P(("groups", "attn")),
            P(("groups", "attn"), None),
            P(("groups", "attn"), "expert"),
            P("expert"),
            P(("groups", "attn"), None),
            P(("groups", "attn"), None),
            P("expert", None, "attn"),
            P("expert", None, "attn"),
            P("expert", "attn", None),
            P(("groups", "attn"), None),
            P(("groups", "attn"), None),
        ),
        out_specs=(P(("groups", "attn"), "expert"), P(("groups", "attn"), None, "expert")),
        check_vma=False,
    )
```

```python
import functools

import jax
import jax.numpy as jnp
from jax import lax
from jax.experimental import pallas as pl
from jax.experimental.pallas import tpu as pltpu
from jax.sharding import PartitionSpec as P

D = 6144
HD = 128
PAGE = 16
CAP = 12
EPSILON = 1e-05
HALF = D // 2
QUARTER = D // 4
LO = 8
SLOT_COLS = HALF + QUARTER
LANES = 128
SCORE_SCALE = HD ** (-0.5)
NEG = -(2.0**100)
F32 = jnp.float32
BF16 = jnp.bfloat16
VMEM = pl.BlockSpec(memory_space=pltpu.VMEM)
SMEM = pl.BlockSpec(memory_space=pltpu.SMEM)
HBM = pl.BlockSpec(memory_space=pltpu.HBM)


def iota(shape, dim):
    return lax.broadcasted_iota(jnp.int32, shape, dim)


def eye(size):
    return iota((size, size), 0) == iota((size, size), 1)


def to_column(row, size):
    return jnp.sum(jnp.where(eye(size), row, 0.0), axis=1, keepdims=True)


def to_row(column, size):
    return jnp.sum(jnp.where(eye(size), column, 0.0), axis=0, keepdims=True)


def dot(a, b):
    return lax.dot_general(a, b, (((1,), (0,)), ((), ())), preferred_element_type=F32)


def dot_t(a, b):
    return lax.dot_general(a, b, (((1,), (1,)), ((), ())), preferred_element_type=F32)


def members(routes, expert):
    return jnp.max(jnp.where(routes == expert, 1.0, 0.0), axis=0, keepdims=True)


def mix_slots(shape, dim, part):
    index = iota(shape, dim)
    here = (index >= 4 * part) & (index < 4 * part + 4)
    return jnp.where(here, index - 4 * part + LO, -1).astype(F32)


def split_three(value):
    high = value.astype(BF16)
    rest = value - high.astype(F32)
    middle = rest.astype(BF16)
    low = (rest - middle.astype(F32)).astype(BF16)
    return high.astype(F32), middle.astype(F32), low.astype(F32)


def load(sources, held, sems, small):
    copies = [pltpu.make_async_copy(a, b, sems.at[k]) for k, (a, b) in enumerate(zip(sources[:-1], held[:-1]))]
    pool = held[-1]
    for head in range(pool.shape[1] // (2 * HD)):
        columns = pl.ds(2 * head * HD, 2 * HD)
        copies.append(
            pltpu.make_async_copy(sources[-1].at[:, columns], pool.at[:, columns], sems.at[len(sources) - 1 + head])
        )
    for copy in copies:
        copy.start()
    for copy in copies[:small]:
        copy.wait()
    return copies[small:]


def tokens_held(counts, tails, rows, pages):
    counts_row = counts[...].astype(F32)
    row_a, row_b = iota((rows, rows), 0), iota((rows, rows), 1)
    first = jnp.sum(jnp.where(row_b < row_a, counts_row, 0.0), axis=1, keepdims=True)
    count = to_column(counts_row, rows)
    tail = to_column(tails[...].astype(F32), rows)
    place = iota((rows, pages), 1).astype(F32)
    inside = (place >= first) & (place < first + count)
    return jnp.where(inside, jnp.where(place == first + count - 1.0, tail, float(PAGE)), 0.0)


def hide_foreign(held, order, tokens):
    rows, pages = held.shape
    page_at = to_column(order[...].astype(F32), pages)
    page_of = (iota((pages, tokens), 1) // PAGE).astype(F32)
    placed = jnp.where(page_at == page_of, 1.0, 0.0).astype(BF16)
    limit = dot(held.astype(BF16), placed)
    visible = (iota((rows, tokens), 1) % PAGE).astype(F32) < limit
    return jnp.where(visible, 0.0, NEG)


def attend(query_of, newest, pool, penalty, waits, finish):
    rows, tokens = penalty.shape
    heads_here = pool.shape[1] // (2 * HD)
    own_penalty = jnp.where(eye(rows), 0.0, NEG)
    products = []
    for head in range(heads_here):
        if head % 2 == 0:
            for copy in waits[head : head + 2]:
                copy.wait()
        keys = slice(2 * head * HD, (2 * head + 1) * HD)
        query = query_of(head)
        group = query.shape[0] // rows
        scores = dot_t(query, pool[:, keys]).reshape(group, rows, tokens) + penalty[None]
        own = dot_t(query, newest[:, keys]).reshape(group, rows, rows) + own_penalty[None]
        products.append((scores.reshape(group * rows, tokens), own.reshape(group * rows, rows)))
    for head, (scores, own) in enumerate(products):
        values = slice((2 * head + 1) * HD, (2 * head + 2) * HD)
        top = jnp.maximum(jnp.max(scores, axis=1, keepdims=True), jnp.max(own, axis=1, keepdims=True))
        weights = jnp.exp((scores - top) * SCORE_SCALE)
        own_weights = jnp.exp((own - top) * SCORE_SCALE)
        total = jnp.sum(weights, axis=1, keepdims=True) + jnp.sum(own_weights, axis=1, keepdims=True)
        inverse = 1.0 / total
        mixed = dot((weights * inverse).astype(BF16), pool[:, values])
        mixed = mixed + dot((own_weights * inverse).astype(BF16), newest[:, values])
        for g in range(group):
            at = (head * group + g) * HD
            finish(slice(at, at + HD), mixed[g * rows : (g + 1) * rows])


def hidden_kernel(*refs):
    sources, hidden, held, sems = refs[:7], refs[7], refs[8:15], refs[15]
    counts, tails, order, queries, new_kv, residual, pool = held
    waits = load(sources, held, sems, 3)
    rows, tokens = queries.shape[0], pool.shape[0]
    penalty = hide_foreign(tokens_held(counts, tails, rows, tokens // PAGE), order, tokens)
    for copy in waits[:3]:
        copy.wait()
    heads_here = pool.shape[1] // (2 * HD)
    group = queries.shape[1] // (heads_here * HD)

    def query_of(head):
        base = head * group * HD
        return jnp.concatenate([queries[:, base + g * HD : base + (g + 1) * HD] for g in range(group)], axis=0)

    def finish(columns, attended):
        hidden[:, columns] = residual[:, columns].astype(F32) + attended

    attend(query_of, new_kv, pool, penalty, waits[3:], finish)


def slots_kernel(hosted, *refs):
    sources, (kept, other), held, (hidden, sems) = refs[:11], refs[11:13], refs[13:24], refs[24:]
    counts, tails, order, routes, mig_pages, mig_dest, queries, new_kv, residual, gain, pool = held
    waits = load(sources, held, sems, 6)
    rows, tokens = queries.shape[0], pool.shape[0]
    heads_here = pool.shape[1] // (2 * HD)
    group = queries.shape[1] // (heads_here * HD)

    row_a, row_b = iota((rows, rows), 0), iota((rows, rows), 1)
    maps, mixed = [], None
    for expert in range(hosted):
        member_row = members(routes[...], expert)
        rank = jnp.sum(jnp.where(row_a <= row_b, to_column(member_row, rows), 0.0), axis=0, keepdims=True) - 1.0
        rank = jnp.where(member_row > 0.0, rank, -2.0)
        maps.append(jnp.where(rank == iota((LO, rows), 0).astype(F32), 1.0, 0.0))
        part = jnp.where(rank == mix_slots((LO, rows), 0, expert), 1.0, 0.0)
        mixed = part if mixed is None else mixed + part
    chosen = jnp.concatenate(maps + [mixed], axis=0).astype(BF16)
    slots = chosen.shape[0]
    held_here = dot(chosen, tokens_held(counts, tails, rows, tokens // PAGE).astype(BF16))
    penalty = hide_foreign(held_here, order, tokens)
    for copy in waits[:4]:
        copy.wait()
    newest = dot(chosen, new_kv[...]).astype(BF16)
    hidden[...] = dot(chosen, residual[...])
    squares = [jnp.zeros((slots, HD), F32)]

    def query_of(head):
        picked = dot(chosen, queries[:, head * group * HD : (head + 1) * group * HD])
        return jnp.concatenate([picked[:, g * HD : (g + 1) * HD] for g in range(group)], axis=0).astype(BF16)

    def finish(columns, attended):
        part = hidden[:, columns] + attended
        hidden[:, columns] = part * gain[:, columns]
        squares[0] = squares[0] + part * part

    attend(query_of, newest, pool, penalty, waits[4:], finish)

    sums = jnp.sum(squares[0], axis=1, keepdims=True) + jnp.zeros((slots, LANES), F32)
    upper = iota((LO, 1), 0) < 4
    tail_rows, tail_sums = hidden[hosted * LO :, :], sums[hosted * LO :]
    lane = iota((LO, LANES), 1)
    by_expert = []
    for expert in range(hosted):

        def spread(first, second):
            if expert == 0:
                return jnp.where(upper, first, pltpu.roll(second, 4, 0))
            return jnp.where(upper, pltpu.roll(first, 4, 0), second)

        low = hidden[expert * LO : (expert + 1) * LO, :]
        mix = spread(tail_rows[:, :QUARTER], tail_rows[:, QUARTER:])
        extra = jnp.zeros((LO, LANES), F32)
        pieces = split_three(sums[expert * LO : (expert + 1) * LO]) + split_three(spread(tail_sums, tail_sums))
        for at, piece in enumerate(pieces):
            extra = jnp.where(lane == at, piece, extra)
        by_expert.append(jnp.concatenate([low, mix, extra], axis=1))
    first_half = lax.axis_index("expert") == 0
    extra_at = SLOT_COLS + LANES
    mine = jnp.where(first_half, by_expert[0], by_expert[1])
    kept[:, :extra_at] = jnp.concatenate([mine, jnp.zeros_like(mine)], axis=0).astype(BF16)
    other[...] = jnp.where(first_half, by_expert[1], by_expert[0]).astype(BF16)

    entries = mig_pages.shape[1]
    page_width = pool.shape[1]
    lane = iota((PAGE, LANES), 1)
    notes = jnp.where(lane == entries, lax.axis_index("attn").astype(F32), 0.0)
    for entry in range(entries):
        start = pl.multiple_of(mig_pages[0, entry] * PAGE, PAGE)
        at = extra_at + entry * page_width
        kept[:, at : at + page_width] = pool[pl.ds(start, PAGE), :]
        notes = jnp.where(lane == entry, mig_dest[0, entry].astype(F32), notes)
    kept[:, extra_at + entries * page_width :] = notes.astype(BF16)


def pack_kernel(kept, theirs, message):
    lane = iota((LO, LANES), 1)
    mine = kept[:, : SLOT_COLS + LANES].astype(F32)[:LO]
    extra = mine[:, SLOT_COLS:] + theirs[:, SLOT_COLS:].astype(F32)
    low_scale = lax.rsqrt(jnp.sum(jnp.where(lane < 3, extra, 0.0), axis=1, keepdims=True) / D + EPSILON)
    mix_sum = jnp.sum(jnp.where((lane >= 3) & (lane < 6), extra, 0.0), axis=1, keepdims=True)
    mix_scale = lax.rsqrt(mix_sum / D + EPSILON)
    first_half = lax.axis_index("expert") == 0
    for columns, scale in ((slice(0, HALF), low_scale), (slice(HALF, SLOT_COLS), mix_scale)):
        a = mine[:, columns] * scale
        b = theirs[:, columns].astype(F32) * scale
        both = jnp.concatenate([jnp.where(first_half, a, b), jnp.where(first_half, b, a)], axis=0)
        message[:, columns] = both.astype(BF16)
    message[:, SLOT_COLS:] = kept[:, SLOT_COLS + LANES :]


def copy_kernel(source, out):
    out[...] = source[...]


def fetch_kernel(source, out, sem):
    copy = pltpu.make_async_copy(source, out, sem)
    copy.start()
    copy.wait()


def ffn_kernel(cut, *refs):
    count = len(refs) // 2 - 3 if cut is None else 1
    pieces = count if cut is None else 2
    blocks, (gate, up, down) = refs[:pieces], refs[pieces : pieces + 3]
    outs = refs[pieces + 3 : pieces + 3 + count]
    low_rows, mix_rows, gate_sum, up_sum = refs[pieces + 3 + count :]
    if cut is None:
        for j in range(count):
            low_rows[16 * j : 16 * j + 16, :] = blocks[j][:, :HALF]
            mix_rows[16 * j : 16 * j + 16, :] = blocks[j][:, HALF:SLOT_COLS]
    else:
        low_rows[...] = blocks[0][:, :HALF]
        mix_rows[:, : cut - HALF] = blocks[0][:, HALF:cut]
        mix_rows[:, cut - HALF :] = blocks[1][:, : SLOT_COLS - cut]

    groups = [(first, min(8, count - first)) for first in range(0, count, 8)]
    width = gate.shape[1]
    for q in range(4):
        part = slice(q * QUARTER, (q + 1) * QUARTER)
        within = slice((q % 2) * QUARTER, (q % 2 + 1) * QUARTER)
        for first, size in groups:
            at, span = 16 * first, 16 * size
            row = iota((span, 1), 0) % 16
            low_here, mix_here = (row // 8) == q // 2, (row // 4) == q
            left = jnp.concatenate([low_rows[at : at + span, within], mix_rows[at : at + span, :]], axis=0)
            for weight, total in ((gate, gate_sum), (up, up_sum)):
                product = dot(left, weight[part, :])
                low = jnp.where(low_here, product[:span], 0.0)
                mix = jnp.where(mix_here, product[span:], 0.0)
                if q == 0:
                    total[0, at : at + span, :] = low
                    total[1, at : at + span, :] = mix
                else:
                    total[0, at : at + span, :] += low
                    total[1, at : at + span, :] += mix

    def fold(total, at, size):
        low, mix = [
            jnp.sum(total[k, at : at + 16 * size, :].reshape(size, 2, 8, width), axis=1).reshape(8 * size, width)
            for k in range(2)
        ]
        lower = iota((8 * size, 1), 0) % 8 < 4
        other = jnp.where(lower, pltpu.roll(mix, 8 * size - 4, 0), pltpu.roll(mix, 4, 0))
        return low, mix + other

    first_rows = iota((8, 1), 0) < 4
    for first, size in groups:
        at = 16 * first
        pieces = [jax.nn.silu(g) * u for g, u in zip(fold(gate_sum, at, size), fold(up_sum, at, size))]
        active = jnp.concatenate([p.reshape(size, 8, width) for p in pieces], axis=1)
        active = active.reshape(16 * size, width).astype(BF16)
        quarters = [dot(active, down[:, q * QUARTER : (q + 1) * QUARTER]) for q in range(4)]
        for j in range(size):
            out = outs[first + j]
            low_at, mix_at = slice(16 * j, 16 * j + 8), slice(16 * j + 8, 16 * j + 16)
            for part in range(2):
                both = jnp.concatenate([quarters[part][low_at], quarters[2 + part][low_at]], axis=0)
                out[:, part * QUARTER : (part + 1) * QUARTER] = both.astype(BF16)
            both = jnp.concatenate(
                [jnp.where(first_rows, quarters[k][mix_at], quarters[k + 1][mix_at]) for k in (0, 2)], axis=0
            )
            out[:, HALF:] = both.astype(BF16)


def arrive_kernel(n, cut, page_width, *refs):
    blocks, (arrived, board, board_smem, sem) = refs[: n + 1], refs[n + 1 :]
    entries = arrived.shape[0]
    notes_at = SLOT_COLS + entries * page_width
    heads = [block[:, notes_at:].astype(F32)[0:1] for block in blocks[: n - 1]]
    heads.append(blocks[n][:, notes_at - cut :].astype(F32)[0:1])
    notes = jnp.concatenate(heads, axis=0)
    lane = iota((n, LANES), 1)
    match = (notes == lax.axis_index("attn").astype(F32)) & (lane < entries)
    named = jnp.max(jnp.where(match, 1.0, 0.0), axis=1, keepdims=True)
    source = jnp.sum(jnp.where(lane == entries, notes, 0.0), axis=1, keepdims=True)
    earlier = to_row(source, n) < source
    rank = jnp.sum(jnp.where(earlier, to_row(named, n), 0.0), axis=1, keepdims=True)
    board[...] = jnp.where(match, rank, -1.0).astype(jnp.int32)
    copy = pltpu.make_async_copy(board, board_smem, sem)
    copy.start()
    arrived[...] = jnp.zeros_like(arrived)
    copy.wait()
    for j in range(n):
        block, shift = (blocks[j], 0) if j < n - 1 else (blocks[n], cut)
        for entry in range(entries):
            slot = board_smem[j, entry]
            at = SLOT_COLS + entry * page_width - shift

            @pl.when((slot >= 0) & (slot < entries))
            def _():
                arrived[slot] = block[:, at : at + page_width]


def gather_kernel(core, own, arrived, jumped, out):
    extra = jnp.where(lax.axis_index("expert") == core, jumped[...].astype(F32), 0.0)
    out[...] = (own[...].astype(F32) + arrived[...].astype(F32) + extra).astype(BF16)


def finish_kernel(own, from_left, from_right, mine, other):
    total = own[...].astype(F32) + from_left[...].astype(F32) + from_right[...].astype(F32)
    first_half = lax.axis_index("expert") == 0
    top, bottom = total[:LO], total[LO:]
    mine[...] = jnp.where(first_half, top, bottom).astype(BF16)
    other[...] = jnp.where(first_half, bottom, top).astype(BF16)


def combine_kernel(hosted, hidden, mine, theirs, routes, gates, layer_out):
    rows = hidden.shape[0]
    first_half = lax.axis_index("expert") == 0
    a, b = mine[...].astype(F32), theirs[...].astype(F32)
    by_expert = [jnp.where(first_half, a, b).astype(BF16), jnp.where(first_half, b, a).astype(BF16)]
    row_a, row_b = iota((rows, rows), 0), iota((rows, rows), 1)
    terms = [[], []]
    for expert in range(hosted):
        member = members(routes[...], expert)
        share = jnp.sum(jnp.where(routes[...] == expert, gates[...], 0.0), axis=0, keepdims=True)
        share = to_column(share, rows)
        rank = jnp.sum(jnp.where(row_b <= row_a, member, 0.0), axis=1, keepdims=True) - 1.0
        rank = jnp.where(to_column(member, rows) > 0.0, rank, -2.0)
        low = jnp.where(rank == iota((rows, LO), 1).astype(F32), 1.0, 0.0).astype(BF16)
        for part in range(2):
            columns = slice(part * QUARTER, (part + 1) * QUARTER)
            mix = jnp.where(rank == mix_slots((rows, LO), 1, part), 1.0, 0.0).astype(BF16)
            value = dot(low, by_expert[expert][:, columns]) + dot(mix, by_expert[expert][:, HALF:])
            terms[part].append(share * value)
    for part in range(2):
        columns = slice(part * QUARTER, (part + 1) * QUARTER)
        layer_out[:, columns] = (hidden[:, columns] + (terms[part][0] + terms[part][1])).astype(BF16)


def call(kernel, outs, in_specs, args, scratch=(), flops=0, bytes_accessed=0, vmem=16 << 20):
    many = isinstance(outs, (list, tuple))
    return pl.pallas_call(
        kernel,
        out_shape=outs,
        in_specs=in_specs,
        out_specs=[VMEM] * len(outs) if many else VMEM,
        scratch_shapes=list(scratch),
        compiler_params=pltpu.CompilerParams(vmem_limit_bytes=vmem),
        cost_estimate=pl.CostEstimate(flops=flops, bytes_accessed=bytes_accessed, transcendentals=0),
    )(*args)


def ring_order(n):
    return [0, 2, 4, 6, 7, 5, 3, 1] if n == 8 else list(range(n))


def fetch_weight(shape, weight):
    return call(
        fetch_kernel,
        shape(weight.shape, BF16),
        [HBM],
        (weight,),
        scratch=(pltpu.SemaphoreType.DMA,),
        bytes_accessed=6_400_000,
    )


def add(a, b):
    return (a.astype(F32) + b.astype(F32)).astype(BF16)


def per_device(
    n,
    hosted,
    queries,
    new_kv,
    kv_pool,
    page_counts,
    tail_tokens,
    page_order,
    residual,
    norm_gain,
    routes,
    route_gates,
    w_gate,
    w_up,
    w_down,
    mig_pages,
    mig_dest,
):
    rows, width = queries.shape
    page_width = kv_pool.shape[2]
    entries = mig_pages.shape[1]
    pool = kv_pool.reshape(-1, page_width)
    around = ring_order(n)
    right = [(around[i], around[(i + 1) % n]) for i in range(n)]
    left = [(b, a) for a, b in right]
    reach = n // 2 - 1
    jump = [(around[i] * hosted, around[(i + reach) % n] * hosted) for i in range(n)]
    jump += [(around[i] * hosted + 1, around[(i - reach) % n] * hosted + 1) for i in range(n)]
    swap = [(0, 1), (1, 0)]
    shape = jax.ShapeDtypeStruct

    moved_cols = entries * page_width + LANES
    lengths = (page_counts, tail_tokens.reshape(1, -1), page_order)
    spaces = {mig_pages.shape: pltpu.SMEM}

    def attention(kernel, outs, sources, scratch, flops):
        held = [spaces.get(x.shape, pltpu.VMEM)(x.shape, x.dtype) for x in sources]
        sems = pltpu.SemaphoreType.DMA((len(sources) + page_width // (2 * HD),))
        return call(
            kernel,
            outs,
            [HBM] * len(sources),
            sources,
            scratch=held + scratch + [sems],
            flops=flops,
            bytes_accessed=3_500_000,
            vmem=60 << 20,
        )

    kept, other = attention(
        functools.partial(slots_kernel, hosted),
        [shape((2 * LO, SLOT_COLS + LANES + moved_cols), BF16), shape((LO, SLOT_COLS + LANES), BF16)],
        (*lengths, routes.T, mig_pages, mig_dest, queries, new_kv, residual, norm_gain.reshape(1, -1), pool),
        [pltpu.VMEM((2 * CAP, width), F32)],
        400_000_000,
    )
    tie = lax.optimization_barrier
    theirs = lax.ppermute(other, "expert", swap)
    kept = call(copy_kernel, shape(kept.shape, BF16), [VMEM], (kept,), bytes_accessed=3_000_000)
    theirs, kept = tie((theirs, kept))
    message = call(
        pack_kernel,
        shape((2 * LO, SLOT_COLS + moved_cols), BF16),
        [VMEM] * 2,
        (kept, theirs),
        flops=500_000,
        bytes_accessed=500_000,
    )

    far = n // 2
    cut = HALF + 3 * LANES
    fetch = functools.partial(fetch_weight, shape)
    from_left, from_right = [message], [message]
    weights, stored = [], [w_gate[0], w_up[0], w_down[0]]
    for step in range(far):
        a, b = from_left[-1], from_right[-1]
        if step == far - 1:
            a, b = a[:, :cut], b[:, cut:]
        a, b = lax.ppermute(a, "attn", right), lax.ppermute(b, "attn", left)
        if step == 0:
            hidden = attention(
                hidden_kernel,
                shape((rows, width), F32),
                (*lengths, queries, new_kv, residual, pool),
                [],
                4_000_000_000,
            )
            b, hidden = tie((b, hidden))
        else:
            for weight in stored[2 * step - 2 : 2 * step]:
                weights.append(fetch(weight))
                a, weights[-1] = tie((a, weights[-1]))
        from_left.append(a)
        from_right.append(b)
    last_a, last_b = from_left.pop(), from_right.pop()
    blocks = [message] + from_left[1:] + from_right[1:]
    ff = w_gate.shape[2]

    def feed_forward(pieces, count, cut):
        return call(
            functools.partial(ffn_kernel, cut),
            [shape((2 * LO, SLOT_COLS), BF16)] * count,
            [VMEM] * (len(pieces) + 3),
            (*pieces, *weights),
            scratch=(
                pltpu.VMEM((16 * count, HALF), BF16),
                pltpu.VMEM((16 * count, QUARTER), BF16),
                pltpu.VMEM((2, 16 * count, ff), F32),
                pltpu.VMEM((2, 16 * count, ff), F32),
            ),
            flops=2_000_000_000,
            bytes_accessed=8_000_000,
        )

    outs = list(feed_forward(blocks, n - 1, None))
    to_left = {k: outs[k] for k in range(1, far)}
    to_right = {k: outs[far - 1 + k] for k in range(1, far)}
    going_right = going_left = jumped = None

    def gather(core, *terms):
        return call(
            functools.partial(gather_kernel, core),
            shape((2 * LO, SLOT_COLS), BF16),
            [VMEM] * 3,
            terms,
            flops=300_000,
            bytes_accessed=600_000,
        )

    for k in range(far - 1, 0, -1):
        send_right, send_left = to_right[k], to_left[k]
        if k == 1:
            send_right, send_left = gather(0, send_right, going_right, jumped), gather(1, send_left, going_left, jumped)
        elif k < far - 1:
            send_right, send_left = add(send_right, going_right), add(send_left, going_left)
        going_right = lax.ppermute(send_right, "attn", right)
        going_left = lax.ppermute(send_left, "attn", left)
        if k == far - 1:
            (opposite,) = feed_forward((last_a, last_b), 1, cut)
            going_right, opposite = tie((going_right, opposite))
            jumped = lax.ppermute(opposite, ("attn", "expert"), jump)
        if k == far - 2:
            arrived = call(
                functools.partial(arrive_kernel, n, cut, page_width),
                shape((entries, PAGE, page_width), BF16),
                [VMEM] * (n + 1),
                (*blocks, last_a, last_b),
                scratch=(
                    pltpu.VMEM((n, LANES), jnp.int32),
                    pltpu.SMEM((n, LANES), jnp.int32),
                    pltpu.SemaphoreType.DMA,
                ),
                flops=100_000,
                bytes_accessed=2_000_000,
            )
            going_left, arrived = tie((going_left, arrived))
    kept, other_half = call(
        finish_kernel,
        [shape((LO, SLOT_COLS), BF16)] * 2,
        [VMEM] * 3,
        (outs[0], going_right, going_left),
        flops=500_000,
        bytes_accessed=600_000,
    )
    returned = lax.ppermute(other_half, "expert", swap)
    layer_out = call(
        functools.partial(combine_kernel, hosted),
        shape((rows, width), BF16),
        [VMEM] * 5,
        (hidden, kept, returned, routes.T, route_gates.T),
        flops=20_000_000,
        bytes_accessed=800_000,
    )
    return layer_out, arrived


def solution(mesh):
    n, hosted = mesh.shape["attn"], mesh.shape["expert"]
    return jax.shard_map(
        functools.partial(per_device, n, hosted),
        mesh=mesh,
        in_specs=(
            P(("groups", "attn"), "expert"),
            P(("groups", "attn"), "expert"),
            P(("groups", "attn"), None, "expert"),
            P(("groups", "attn"), None),
            P(("groups", "attn")),
            P(("groups", "attn"), None),
            P(("groups", "attn"), "expert"),
            P("expert"),
            P(("groups", "attn"), None),
            P(("groups", "attn"), None),
            P("expert", None, "attn"),
            P("expert", None, "attn"),
            P("expert", "attn", None),
            P(("groups", "attn"), None),
            P(("groups", "attn"), None),
        ),
        out_specs=(P(("groups", "attn"), "expert"), P(("groups", "attn"), None, "expert")),
        check_vma=False,
    )
```

```python
import functools

import jax
import jax.numpy as jnp
from jax import lax
from jax.experimental import pallas as pl
from jax.experimental.pallas import tpu as pltpu
from jax.sharding import PartitionSpec as P

D = 6144
HD = 128
PAGE = 16
CAP = 12
EPSILON = 1e-05
HALF = D // 2
QUARTER = D // 4
LO = 8
SLOT_COLS = HALF + QUARTER
LANES = 128
SCORE_SCALE = HD ** (-0.5)
NEG = -(2.0**100)
F32 = jnp.float32
BF16 = jnp.bfloat16
VMEM = pl.BlockSpec(memory_space=pltpu.VMEM)
SMEM = pl.BlockSpec(memory_space=pltpu.SMEM)
HBM = pl.BlockSpec(memory_space=pltpu.HBM)


def iota(shape, dim):
    return lax.broadcasted_iota(jnp.int32, shape, dim)


def eye(size):
    return iota((size, size), 0) == iota((size, size), 1)


def to_column(row, size):
    return jnp.sum(jnp.where(eye(size), row, 0.0), axis=1, keepdims=True)


def to_row(column, size):
    return jnp.sum(jnp.where(eye(size), column, 0.0), axis=0, keepdims=True)


def dot(a, b):
    return lax.dot_general(a, b, (((1,), (0,)), ((), ())), preferred_element_type=F32)


def dot_t(a, b):
    return lax.dot_general(a, b, (((1,), (1,)), ((), ())), preferred_element_type=F32)


def members(routes, expert):
    return jnp.max(jnp.where(routes == expert, 1.0, 0.0), axis=0, keepdims=True)


def mix_slots(shape, dim, part):
    index = iota(shape, dim)
    here = (index >= 4 * part) & (index < 4 * part + 4)
    return jnp.where(here, index - 4 * part + LO, -1).astype(F32)


def split_three(value):
    high = value.astype(BF16)
    rest = value - high.astype(F32)
    middle = rest.astype(BF16)
    low = (rest - middle.astype(F32)).astype(BF16)
    return high.astype(F32), middle.astype(F32), low.astype(F32)


def load(sources, held, sems, small):
    copies = [pltpu.make_async_copy(a, b, sems.at[k]) for k, (a, b) in enumerate(zip(sources[:-1], held[:-1]))]
    pool = held[-1]
    for head in range(pool.shape[1] // (2 * HD)):
        columns = pl.ds(2 * head * HD, 2 * HD)
        copies.append(
            pltpu.make_async_copy(sources[-1].at[:, columns], pool.at[:, columns], sems.at[len(sources) - 1 + head])
        )
    for copy in copies:
        copy.start()
    for copy in copies[:small]:
        copy.wait()
    return copies[small:]


def tokens_held(counts, tails, rows, pages):
    counts_row = counts[...].astype(F32)
    row_a, row_b = iota((rows, rows), 0), iota((rows, rows), 1)
    first = jnp.sum(jnp.where(row_b < row_a, counts_row, 0.0), axis=1, keepdims=True)
    count = to_column(counts_row, rows)
    tail = to_column(tails[...].astype(F32), rows)
    place = iota((rows, pages), 1).astype(F32)
    inside = (place >= first) & (place < first + count)
    return jnp.where(inside, jnp.where(place == first + count - 1.0, tail, float(PAGE)), 0.0)


def hide_foreign(held, order, tokens):
    rows, pages = held.shape
    page_at = to_column(order[...].astype(F32), pages)
    page_of = (iota((pages, tokens), 1) // PAGE).astype(F32)
    placed = jnp.where(page_at == page_of, 1.0, 0.0).astype(BF16)
    limit = dot(held.astype(BF16), placed)
    visible = (iota((rows, tokens), 1) % PAGE).astype(F32) < limit
    return jnp.where(visible, 0.0, NEG)


def attend(query_of, newest, pool, penalty, waits, finish):
    rows, tokens = penalty.shape
    heads_here = pool.shape[1] // (2 * HD)
    own_penalty = jnp.where(eye(rows), 0.0, NEG)
    products = []
    for head in range(heads_here):
        if head % 2 == 0:
            for copy in waits[head : head + 2]:
                copy.wait()
        keys = slice(2 * head * HD, (2 * head + 1) * HD)
        query = query_of(head)
        group = query.shape[0] // rows
        scores = dot_t(query, pool[:, keys]).reshape(group, rows, tokens) + penalty[None]
        own = dot_t(query, newest[:, keys]).reshape(group, rows, rows) + own_penalty[None]
        products.append((scores.reshape(group * rows, tokens), own.reshape(group * rows, rows)))
    for head, (scores, own) in enumerate(products):
        values = slice((2 * head + 1) * HD, (2 * head + 2) * HD)
        top = jnp.maximum(jnp.max(scores, axis=1, keepdims=True), jnp.max(own, axis=1, keepdims=True))
        weights = jnp.exp((scores - top) * SCORE_SCALE)
        own_weights = jnp.exp((own - top) * SCORE_SCALE)
        total = jnp.sum(weights, axis=1, keepdims=True) + jnp.sum(own_weights, axis=1, keepdims=True)
        inverse = 1.0 / total
        mixed = dot((weights * inverse).astype(BF16), pool[:, values])
        mixed = mixed + dot((own_weights * inverse).astype(BF16), newest[:, values])
        for g in range(group):
            at = (head * group + g) * HD
            finish(slice(at, at + HD), mixed[g * rows : (g + 1) * rows])


def hidden_kernel(*refs):
    sources, hidden, held, sems = refs[:7], refs[7], refs[8:15], refs[15]
    counts, tails, order, queries, new_kv, residual, pool = held
    waits = load(sources, held, sems, 3)
    rows, tokens = queries.shape[0], pool.shape[0]
    penalty = hide_foreign(tokens_held(counts, tails, rows, tokens // PAGE), order, tokens)
    for copy in waits[:3]:
        copy.wait()
    heads_here = pool.shape[1] // (2 * HD)
    group = queries.shape[1] // (heads_here * HD)

    def query_of(head):
        base = head * group * HD
        return jnp.concatenate([queries[:, base + g * HD : base + (g + 1) * HD] for g in range(group)], axis=0)

    def finish(columns, attended):
        hidden[:, columns] = residual[:, columns].astype(F32) + attended

    attend(query_of, new_kv, pool, penalty, waits[3:], finish)


def slots_kernel(hosted, *refs):
    sources, (kept, other), held, (hidden, sems) = refs[:11], refs[11:13], refs[13:24], refs[24:]
    counts, tails, order, routes, mig_pages, mig_dest, queries, new_kv, residual, gain, pool = held
    waits = load(sources, held, sems, 6)
    rows, tokens = queries.shape[0], pool.shape[0]
    heads_here = pool.shape[1] // (2 * HD)
    group = queries.shape[1] // (heads_here * HD)

    row_a, row_b = iota((rows, rows), 0), iota((rows, rows), 1)
    maps, mixed = [], None
    for expert in range(hosted):
        member_row = members(routes[...], expert)
        rank = jnp.sum(jnp.where(row_a <= row_b, to_column(member_row, rows), 0.0), axis=0, keepdims=True) - 1.0
        rank = jnp.where(member_row > 0.0, rank, -2.0)
        maps.append(jnp.where(rank == iota((LO, rows), 0).astype(F32), 1.0, 0.0))
        part = jnp.where(rank == mix_slots((LO, rows), 0, expert), 1.0, 0.0)
        mixed = part if mixed is None else mixed + part
    chosen = jnp.concatenate(maps + [mixed], axis=0).astype(BF16)
    slots = chosen.shape[0]
    held_here = dot(chosen, tokens_held(counts, tails, rows, tokens // PAGE).astype(BF16))
    penalty = hide_foreign(held_here, order, tokens)
    for copy in waits[:4]:
        copy.wait()
    newest = dot(chosen, new_kv[...]).astype(BF16)
    hidden[...] = dot(chosen, residual[...])
    squares = [jnp.zeros((slots, HD), F32)]

    def query_of(head):
        picked = dot(chosen, queries[:, head * group * HD : (head + 1) * group * HD])
        return jnp.concatenate([picked[:, g * HD : (g + 1) * HD] for g in range(group)], axis=0).astype(BF16)

    def finish(columns, attended):
        part = hidden[:, columns] + attended
        hidden[:, columns] = part * gain[:, columns]
        squares[0] = squares[0] + part * part

    attend(query_of, newest, pool, penalty, waits[4:], finish)

    sums = jnp.sum(squares[0], axis=1, keepdims=True) + jnp.zeros((slots, LANES), F32)
    upper = iota((LO, 1), 0) < 4
    tail_rows, tail_sums = hidden[hosted * LO :, :], sums[hosted * LO :]
    lane = iota((LO, LANES), 1)
    by_expert = []
    for expert in range(hosted):

        def spread(first, second):
            if expert == 0:
                return jnp.where(upper, first, pltpu.roll(second, 4, 0))
            return jnp.where(upper, pltpu.roll(first, 4, 0), second)

        low = hidden[expert * LO : (expert + 1) * LO, :]
        mix = spread(tail_rows[:, :QUARTER], tail_rows[:, QUARTER:])
        extra = jnp.zeros((LO, LANES), F32)
        pieces = split_three(sums[expert * LO : (expert + 1) * LO]) + split_three(spread(tail_sums, tail_sums))
        for at, piece in enumerate(pieces):
            extra = jnp.where(lane == at, piece, extra)
        by_expert.append(jnp.concatenate([low, mix, extra], axis=1))
    first_half = lax.axis_index("expert") == 0
    extra_at = SLOT_COLS + LANES
    mine = jnp.where(first_half, by_expert[0], by_expert[1])
    kept[:, :extra_at] = jnp.concatenate([mine, jnp.zeros_like(mine)], axis=0).astype(BF16)
    other[...] = jnp.where(first_half, by_expert[1], by_expert[0]).astype(BF16)

    entries = mig_pages.shape[1]
    page_width = pool.shape[1]
    lane = iota((PAGE, LANES), 1)
    notes = jnp.where(lane == entries, lax.axis_index("attn").astype(F32), 0.0)
    for entry in range(entries):
        start = pl.multiple_of(mig_pages[0, entry] * PAGE, PAGE)
        at = extra_at + entry * page_width
        kept[:, at : at + page_width] = pool[pl.ds(start, PAGE), :]
        notes = jnp.where(lane == entry, mig_dest[0, entry].astype(F32), notes)
    kept[:, extra_at + entries * page_width :] = notes.astype(BF16)


def pack_kernel(kept, theirs, message):
    lane = iota((LO, LANES), 1)
    mine = kept[:, : SLOT_COLS + LANES].astype(F32)[:LO]
    extra = mine[:, SLOT_COLS:] + theirs[:, SLOT_COLS:].astype(F32)
    low_scale = lax.rsqrt(jnp.sum(jnp.where(lane < 3, extra, 0.0), axis=1, keepdims=True) / D + EPSILON)
    mix_sum = jnp.sum(jnp.where((lane >= 3) & (lane < 6), extra, 0.0), axis=1, keepdims=True)
    mix_scale = lax.rsqrt(mix_sum / D + EPSILON)
    first_half = lax.axis_index("expert") == 0
    for columns, scale in ((slice(0, HALF), low_scale), (slice(HALF, SLOT_COLS), mix_scale)):
        a = mine[:, columns] * scale
        b = theirs[:, columns].astype(F32) * scale
        both = jnp.concatenate([jnp.where(first_half, a, b), jnp.where(first_half, b, a)], axis=0)
        message[:, columns] = both.astype(BF16)
    message[:, SLOT_COLS:] = kept[:, SLOT_COLS + LANES :]


def copy_kernel(source, out):
    out[...] = source[...]


def fetch_kernel(source, out, sem):
    copy = pltpu.make_async_copy(source, out, sem)
    copy.start()
    copy.wait()


def ffn_kernel(cut, *refs):
    count = len(refs) // 2 - 3 if cut is None else 1
    pieces = count if cut is None else 2
    blocks, (gate, up, down) = refs[:pieces], refs[pieces : pieces + 3]
    outs = refs[pieces + 3 : pieces + 3 + count]
    low_rows, mix_rows, gate_sum, up_sum = refs[pieces + 3 + count :]
    if cut is None:
        for j in range(count):
            low_rows[16 * j : 16 * j + 16, :] = blocks[j][:, :HALF]
            mix_rows[16 * j : 16 * j + 16, :] = blocks[j][:, HALF:SLOT_COLS]
    else:
        low_rows[...] = blocks[0][:, :HALF]
        mix_rows[:, : cut - HALF] = blocks[0][:, HALF:cut]
        mix_rows[:, cut - HALF :] = blocks[1][:, : SLOT_COLS - cut]

    groups = [(first, min(8, count - first)) for first in range(0, count, 8)]
    width = gate.shape[1]
    for q in range(4):
        part = slice(q * QUARTER, (q + 1) * QUARTER)
        within = slice((q % 2) * QUARTER, (q % 2 + 1) * QUARTER)
        for first, size in groups:
            at, span = 16 * first, 16 * size
            row = iota((span, 1), 0) % 16
            low_here, mix_here = (row // 8) == q // 2, (row // 4) == q
            left = jnp.concatenate([low_rows[at : at + span, within], mix_rows[at : at + span, :]], axis=0)
            for weight, total in ((gate, gate_sum), (up, up_sum)):
                product = dot(left, weight[part, :])
                low = jnp.where(low_here, product[:span], 0.0)
                mix = jnp.where(mix_here, product[span:], 0.0)
                if q == 0:
                    total[0, at : at + span, :] = low
                    total[1, at : at + span, :] = mix
                else:
                    total[0, at : at + span, :] += low
                    total[1, at : at + span, :] += mix

    def fold(total, at, size):
        low, mix = [
            jnp.sum(total[k, at : at + 16 * size, :].reshape(size, 2, 8, width), axis=1).reshape(8 * size, width)
            for k in range(2)
        ]
        lower = iota((8 * size, 1), 0) % 8 < 4
        other = jnp.where(lower, pltpu.roll(mix, 8 * size - 4, 0), pltpu.roll(mix, 4, 0))
        return low, mix + other

    first_rows = iota((8, 1), 0) < 4
    for first, size in groups:
        at = 16 * first
        pieces = [jax.nn.silu(g) * u for g, u in zip(fold(gate_sum, at, size), fold(up_sum, at, size))]
        active = jnp.concatenate([p.reshape(size, 8, width) for p in pieces], axis=1)
        active = active.reshape(16 * size, width).astype(BF16)
        quarters = [dot(active, down[:, q * QUARTER : (q + 1) * QUARTER]) for q in range(4)]
        for j in range(size):
            out = outs[first + j]
            low_at, mix_at = slice(16 * j, 16 * j + 8), slice(16 * j + 8, 16 * j + 16)
            for part in range(2):
                both = jnp.concatenate([quarters[part][low_at], quarters[2 + part][low_at]], axis=0)
                out[:, part * QUARTER : (part + 1) * QUARTER] = both.astype(BF16)
            both = jnp.concatenate(
                [jnp.where(first_rows, quarters[k][mix_at], quarters[k + 1][mix_at]) for k in (0, 2)], axis=0
            )
            out[:, HALF:] = both.astype(BF16)


def arrive_kernel(n, cut, page_width, *refs):
    blocks, (arrived, board, board_smem, sem) = refs[: n + 1], refs[n + 1 :]
    entries = arrived.shape[0]
    notes_at = SLOT_COLS + entries * page_width
    heads = [block[:, notes_at:].astype(F32)[0:1] for block in blocks[: n - 1]]
    heads.append(blocks[n][:, notes_at - cut :].astype(F32)[0:1])
    notes = jnp.concatenate(heads, axis=0)
    lane = iota((n, LANES), 1)
    match = (notes == lax.axis_index("attn").astype(F32)) & (lane < entries)
    named = jnp.max(jnp.where(match, 1.0, 0.0), axis=1, keepdims=True)
    source = jnp.sum(jnp.where(lane == entries, notes, 0.0), axis=1, keepdims=True)
    earlier = to_row(source, n) < source
    rank = jnp.sum(jnp.where(earlier, to_row(named, n), 0.0), axis=1, keepdims=True)
    board[...] = jnp.where(match, rank, -1.0).astype(jnp.int32)
    copy = pltpu.make_async_copy(board, board_smem, sem)
    copy.start()
    arrived[...] = jnp.zeros_like(arrived)
    copy.wait()
    for j in range(n):
        block, shift = (blocks[j], 0) if j < n - 1 else (blocks[n], cut)
        for entry in range(entries):
            slot = board_smem[j, entry]
            at = SLOT_COLS + entry * page_width - shift

            @pl.when((slot >= 0) & (slot < entries))
            def _():
                arrived[slot] = block[:, at : at + page_width]


def gather_kernel(core, own, arrived, jumped, out):
    extra = jnp.where(lax.axis_index("expert") == core, jumped[...].astype(F32), 0.0)
    out[...] = (own[...].astype(F32) + arrived[...].astype(F32) + extra).astype(BF16)


def finish_kernel(own, from_left, from_right, mine, other):
    total = own[...].astype(F32) + from_left[...].astype(F32) + from_right[...].astype(F32)
    first_half = lax.axis_index("expert") == 0
    top, bottom = total[:LO], total[LO:]
    mine[...] = jnp.where(first_half, top, bottom).astype(BF16)
    other[...] = jnp.where(first_half, bottom, top).astype(BF16)


def combine_kernel(hosted, hidden, mine, theirs, routes, gates, layer_out):
    rows = hidden.shape[0]
    first_half = lax.axis_index("expert") == 0
    a, b = mine[...].astype(F32), theirs[...].astype(F32)
    by_expert = [jnp.where(first_half, a, b).astype(BF16), jnp.where(first_half, b, a).astype(BF16)]
    row_a, row_b = iota((rows, rows), 0), iota((rows, rows), 1)
    terms = [[], []]
    for expert in range(hosted):
        member = members(routes[...], expert)
        share = jnp.sum(jnp.where(routes[...] == expert, gates[...], 0.0), axis=0, keepdims=True)
        share = to_column(share, rows)
        rank = jnp.sum(jnp.where(row_b <= row_a, member, 0.0), axis=1, keepdims=True) - 1.0
        rank = jnp.where(to_column(member, rows) > 0.0, rank, -2.0)
        low = jnp.where(rank == iota((rows, LO), 1).astype(F32), 1.0, 0.0).astype(BF16)
        for part in range(2):
            columns = slice(part * QUARTER, (part + 1) * QUARTER)
            mix = jnp.where(rank == mix_slots((rows, LO), 1, part), 1.0, 0.0).astype(BF16)
            value = dot(low, by_expert[expert][:, columns]) + dot(mix, by_expert[expert][:, HALF:])
            terms[part].append(share * value)
    for part in range(2):
        columns = slice(part * QUARTER, (part + 1) * QUARTER)
        layer_out[:, columns] = (hidden[:, columns] + (terms[part][0] + terms[part][1])).astype(BF16)


def call(kernel, outs, in_specs, args, scratch=(), flops=0, bytes_accessed=0, vmem=16 << 20):
    many = isinstance(outs, (list, tuple))
    return pl.pallas_call(
        kernel,
        out_shape=outs,
        in_specs=in_specs,
        out_specs=[VMEM] * len(outs) if many else VMEM,
        scratch_shapes=list(scratch),
        compiler_params=pltpu.CompilerParams(vmem_limit_bytes=vmem),
        cost_estimate=pl.CostEstimate(flops=flops, bytes_accessed=bytes_accessed, transcendentals=0),
    )(*args)


def ring_order(n):
    return [0, 2, 4, 6, 7, 5, 3, 1] if n == 8 else list(range(n))


def fetch_weight(shape, weight):
    return call(
        fetch_kernel,
        shape(weight.shape, BF16),
        [HBM],
        (weight,),
        scratch=(pltpu.SemaphoreType.DMA,),
        bytes_accessed=6_400_000,
    )


def add(a, b):
    return (a.astype(F32) + b.astype(F32)).astype(BF16)


def per_device(
    n,
    hosted,
    queries,
    new_kv,
    kv_pool,
    page_counts,
    tail_tokens,
    page_order,
    residual,
    norm_gain,
    routes,
    route_gates,
    w_gate,
    w_up,
    w_down,
    mig_pages,
    mig_dest,
):
    rows, width = queries.shape
    page_width = kv_pool.shape[2]
    entries = mig_pages.shape[1]
    pool = kv_pool.reshape(-1, page_width)
    around = ring_order(n)
    right = [(around[i], around[(i + 1) % n]) for i in range(n)]
    left = [(b, a) for a, b in right]
    reach = n // 2 - 1
    jump = [(around[i] * hosted, around[(i + reach) % n] * hosted + 1) for i in range(n)]
    jump += [(around[i] * hosted + 1, around[(i - reach) % n] * hosted) for i in range(n)]
    swap = [(0, 1), (1, 0)]
    shape = jax.ShapeDtypeStruct

    moved_cols = entries * page_width + LANES
    lengths = (page_counts, tail_tokens.reshape(1, -1), page_order)
    spaces = {mig_pages.shape: pltpu.SMEM}

    def attention(kernel, outs, sources, scratch, flops):
        held = [spaces.get(x.shape, pltpu.VMEM)(x.shape, x.dtype) for x in sources]
        sems = pltpu.SemaphoreType.DMA((len(sources) + page_width // (2 * HD),))
        return call(
            kernel,
            outs,
            [HBM] * len(sources),
            sources,
            scratch=held + scratch + [sems],
            flops=flops,
            bytes_accessed=3_500_000,
            vmem=60 << 20,
        )

    kept, other = attention(
        functools.partial(slots_kernel, hosted),
        [shape((2 * LO, SLOT_COLS + LANES + moved_cols), BF16), shape((LO, SLOT_COLS + LANES), BF16)],
        (*lengths, routes.T, mig_pages, mig_dest, queries, new_kv, residual, norm_gain.reshape(1, -1), pool),
        [pltpu.VMEM((2 * CAP, width), F32)],
        400_000_000,
    )
    tie = lax.optimization_barrier
    theirs = lax.ppermute(other, "expert", swap)
    kept = call(copy_kernel, shape(kept.shape, BF16), [VMEM], (kept,), bytes_accessed=3_000_000)
    theirs, kept = tie((theirs, kept))
    message = call(
        pack_kernel,
        shape((2 * LO, SLOT_COLS + moved_cols), BF16),
        [VMEM] * 2,
        (kept, theirs),
        flops=500_000,
        bytes_accessed=500_000,
    )

    far = n // 2
    cut = HALF + 3 * LANES
    fetch = functools.partial(fetch_weight, shape)
    from_left, from_right = [message], [message]
    weights, stored = [], [w_gate[0], w_up[0], w_down[0]]
    for step in range(far):
        a, b = from_left[-1], from_right[-1]
        if step == far - 1:
            a, b = a[:, :cut], b[:, cut:]
        a, b = lax.ppermute(a, "attn", right), lax.ppermute(b, "attn", left)
        if step == 0:
            hidden = attention(
                hidden_kernel,
                shape((rows, width), F32),
                (*lengths, queries, new_kv, residual, pool),
                [],
                4_000_000_000,
            )
            b, hidden = tie((b, hidden))
        else:
            for weight in stored[2 * step - 2 : 2 * step]:
                weights.append(fetch(weight))
                if step == 2:
                    a, weights[-1] = tie((a, weights[-1]))
                else:
                    b, weights[-1] = tie((b, weights[-1]))
        from_left.append(a)
        from_right.append(b)
    last_a, last_b = from_left.pop(), from_right.pop()
    blocks = [message] + from_left[1:] + from_right[1:]
    ff = w_gate.shape[2]

    def feed_forward(pieces, count, cut):
        return call(
            functools.partial(ffn_kernel, cut),
            [shape((2 * LO, SLOT_COLS), BF16)] * count,
            [VMEM] * (len(pieces) + 3),
            (*pieces, *weights),
            scratch=(
                pltpu.VMEM((16 * count, HALF), BF16),
                pltpu.VMEM((16 * count, QUARTER), BF16),
                pltpu.VMEM((2, 16 * count, ff), F32),
                pltpu.VMEM((2, 16 * count, ff), F32),
            ),
            flops=2_000_000_000,
            bytes_accessed=8_000_000,
        )

    outs = list(feed_forward(blocks, n - 1, None))
    to_left = {k: outs[k] for k in range(1, far)}
    to_right = {k: outs[far - 1 + k] for k in range(1, far)}
    going_right = going_left = jumped = None

    def gather(core, *terms):
        return call(
            functools.partial(gather_kernel, core),
            shape((2 * LO, SLOT_COLS), BF16),
            [VMEM] * 3,
            terms,
            flops=300_000,
            bytes_accessed=600_000,
        )

    for k in range(far - 1, 0, -1):
        send_right, send_left = to_right[k], to_left[k]
        if k == 1:
            send_right, send_left = gather(0, send_right, going_right, jumped), gather(1, send_left, going_left, jumped)
        elif k < far - 1:
            send_right, send_left = add(send_right, going_right), add(send_left, going_left)
        going_right = lax.ppermute(send_right, "attn", right)
        going_left = lax.ppermute(send_left, "attn", left)
        if k == far - 1:
            (opposite,) = feed_forward((last_a, last_b), 1, cut)
            going_right, opposite = tie((going_right, opposite))
            jumped = lax.ppermute(lax.ppermute(opposite, ("attn", "expert"), jump), "expert", swap)
        if k == far - 2:
            arrived = call(
                functools.partial(arrive_kernel, n, cut, page_width),
                shape((entries, PAGE, page_width), BF16),
                [VMEM] * (n + 1),
                (*blocks, last_a, last_b),
                scratch=(
                    pltpu.VMEM((n, LANES), jnp.int32),
                    pltpu.SMEM((n, LANES), jnp.int32),
                    pltpu.SemaphoreType.DMA,
                ),
                flops=100_000,
                bytes_accessed=2_000_000,
            )
            going_left, arrived = tie((going_left, arrived))
    kept, other_half = call(
        finish_kernel,
        [shape((LO, SLOT_COLS), BF16)] * 2,
        [VMEM] * 3,
        (outs[0], going_right, going_left),
        flops=500_000,
        bytes_accessed=600_000,
    )
    returned = lax.ppermute(other_half, "expert", swap)
    layer_out = call(
        functools.partial(combine_kernel, hosted),
        shape((rows, width), BF16),
        [VMEM] * 5,
        (hidden, kept, returned, routes.T, route_gates.T),
        flops=20_000_000,
        bytes_accessed=800_000,
    )
    return layer_out, arrived


def solution(mesh):
    n, hosted = mesh.shape["attn"], mesh.shape["expert"]
    return jax.shard_map(
        functools.partial(per_device, n, hosted),
        mesh=mesh,
        in_specs=(
            P(("groups", "attn"), "expert"),
            P(("groups", "attn"), "expert"),
            P(("groups", "attn"), None, "expert"),
            P(("groups", "attn"), None),
            P(("groups", "attn")),
            P(("groups", "attn"), None),
            P(("groups", "attn"), "expert"),
            P("expert"),
            P(("groups", "attn"), None),
            P(("groups", "attn"), None),
            P("expert", None, "attn"),
            P("expert", None, "attn"),
            P("expert", "attn", None),
            P(("groups", "attn"), None),
            P(("groups", "attn"), None),
        ),
        out_specs=(P(("groups", "attn"), "expert"), P(("groups", "attn"), None, "expert")),
        check_vma=False,
    )
```

```python
import functools

import jax
import jax.numpy as jnp
from jax import lax
from jax.experimental import pallas as pl
from jax.experimental.pallas import tpu as pltpu
from jax.sharding import PartitionSpec as P

D = 6144
HD = 128
PAGE = 16
CAP = 12
EPSILON = 1e-05
HALF = D // 2
QUARTER = D // 4
LO = 8
SLOT_COLS = HALF + QUARTER
LANES = 128
SCORE_SCALE = HD ** (-0.5)
NEG = -(2.0**100)
F32 = jnp.float32
BF16 = jnp.bfloat16
VMEM = pl.BlockSpec(memory_space=pltpu.VMEM)
SMEM = pl.BlockSpec(memory_space=pltpu.SMEM)
HBM = pl.BlockSpec(memory_space=pltpu.HBM)


def iota(shape, dim):
    return lax.broadcasted_iota(jnp.int32, shape, dim)


def eye(size):
    return iota((size, size), 0) == iota((size, size), 1)


def to_column(row, size):
    return jnp.sum(jnp.where(eye(size), row, 0.0), axis=1, keepdims=True)


def to_row(column, size):
    return jnp.sum(jnp.where(eye(size), column, 0.0), axis=0, keepdims=True)


def dot(a, b):
    return lax.dot_general(a, b, (((1,), (0,)), ((), ())), preferred_element_type=F32)


def dot_t(a, b):
    return lax.dot_general(a, b, (((1,), (1,)), ((), ())), preferred_element_type=F32)


def members(routes, expert):
    return jnp.max(jnp.where(routes == expert, 1.0, 0.0), axis=0, keepdims=True)


def mix_slots(shape, dim, part):
    index = iota(shape, dim)
    here = (index >= 4 * part) & (index < 4 * part + 4)
    return jnp.where(here, index - 4 * part + LO, -1).astype(F32)


def split_three(value):
    high = value.astype(BF16)
    rest = value - high.astype(F32)
    middle = rest.astype(BF16)
    low = (rest - middle.astype(F32)).astype(BF16)
    return high.astype(F32), middle.astype(F32), low.astype(F32)


def load(sources, held, sems, small):
    copies = [pltpu.make_async_copy(a, b, sems.at[k]) for k, (a, b) in enumerate(zip(sources[:-1], held[:-1]))]
    pool = held[-1]
    for head in range(pool.shape[1] // (2 * HD)):
        columns = pl.ds(2 * head * HD, 2 * HD)
        copies.append(
            pltpu.make_async_copy(sources[-1].at[:, columns], pool.at[:, columns], sems.at[len(sources) - 1 + head])
        )
    for copy in copies:
        copy.start()
    for copy in copies[:small]:
        copy.wait()
    return copies[small:]


def tokens_held(counts, tails, rows, pages):
    counts_row = counts[...].astype(F32)
    row_a, row_b = iota((rows, rows), 0), iota((rows, rows), 1)
    first = jnp.sum(jnp.where(row_b < row_a, counts_row, 0.0), axis=1, keepdims=True)
    count = to_column(counts_row, rows)
    tail = to_column(tails[...].astype(F32), rows)
    place = iota((rows, pages), 1).astype(F32)
    inside = (place >= first) & (place < first + count)
    return jnp.where(inside, jnp.where(place == first + count - 1.0, tail, float(PAGE)), 0.0)


def hide_foreign(held, order, tokens):
    rows, pages = held.shape
    page_at = to_column(order[...].astype(F32), pages)
    page_of = (iota((pages, tokens), 1) // PAGE).astype(F32)
    placed = jnp.where(page_at == page_of, 1.0, 0.0).astype(BF16)
    limit = dot(held.astype(BF16), placed)
    visible = (iota((rows, tokens), 1) % PAGE).astype(F32) < limit
    return jnp.where(visible, 0.0, NEG)


def attend(query_of, newest, pool, penalty, waits, finish):
    rows, tokens = penalty.shape
    heads_here = pool.shape[1] // (2 * HD)
    own_penalty = jnp.where(eye(rows), 0.0, NEG)
    products = []
    for head in range(heads_here):
        if head % 2 == 0:
            for copy in waits[head : head + 2]:
                copy.wait()
        keys = slice(2 * head * HD, (2 * head + 1) * HD)
        query = query_of(head)
        group = query.shape[0] // rows
        scores = dot_t(query, pool[:, keys]).reshape(group, rows, tokens) + penalty[None]
        own = dot_t(query, newest[:, keys]).reshape(group, rows, rows) + own_penalty[None]
        products.append((scores.reshape(group * rows, tokens), own.reshape(group * rows, rows)))
    for head, (scores, own) in enumerate(products):
        values = slice((2 * head + 1) * HD, (2 * head + 2) * HD)
        top = jnp.maximum(jnp.max(scores, axis=1, keepdims=True), jnp.max(own, axis=1, keepdims=True))
        weights = jnp.exp((scores - top) * SCORE_SCALE)
        own_weights = jnp.exp((own - top) * SCORE_SCALE)
        total = jnp.sum(weights, axis=1, keepdims=True) + jnp.sum(own_weights, axis=1, keepdims=True)
        inverse = 1.0 / total
        mixed = dot((weights * inverse).astype(BF16), pool[:, values])
        mixed = mixed + dot((own_weights * inverse).astype(BF16), newest[:, values])
        for g in range(group):
            at = (head * group + g) * HD
            finish(slice(at, at + HD), mixed[g * rows : (g + 1) * rows])


def hidden_kernel(*refs):
    sources, hidden, held, sems = refs[:7], refs[7], refs[8:15], refs[15]
    counts, tails, order, queries, new_kv, residual, pool = held
    waits = load(sources, held, sems, 3)
    rows, tokens = queries.shape[0], pool.shape[0]
    penalty = hide_foreign(tokens_held(counts, tails, rows, tokens // PAGE), order, tokens)
    for copy in waits[:3]:
        copy.wait()
    heads_here = pool.shape[1] // (2 * HD)
    group = queries.shape[1] // (heads_here * HD)

    def query_of(head):
        base = head * group * HD
        return jnp.concatenate([queries[:, base + g * HD : base + (g + 1) * HD] for g in range(group)], axis=0)

    def finish(columns, attended):
        hidden[:, columns] = residual[:, columns].astype(F32) + attended

    attend(query_of, new_kv, pool, penalty, waits[3:], finish)


def slots_kernel(hosted, *refs):
    sources, (kept, other), held, (hidden, sems) = refs[:11], refs[11:13], refs[13:24], refs[24:]
    counts, tails, order, routes, mig_pages, mig_dest, queries, new_kv, residual, gain, pool = held
    waits = load(sources, held, sems, 6)
    rows, tokens = queries.shape[0], pool.shape[0]
    heads_here = pool.shape[1] // (2 * HD)
    group = queries.shape[1] // (heads_here * HD)

    row_a, row_b = iota((rows, rows), 0), iota((rows, rows), 1)
    maps, mixed = [], None
    for expert in range(hosted):
        member_row = members(routes[...], expert)
        rank = jnp.sum(jnp.where(row_a <= row_b, to_column(member_row, rows), 0.0), axis=0, keepdims=True) - 1.0
        rank = jnp.where(member_row > 0.0, rank, -2.0)
        maps.append(jnp.where(rank == iota((LO, rows), 0).astype(F32), 1.0, 0.0))
        part = jnp.where(rank == mix_slots((LO, rows), 0, expert), 1.0, 0.0)
        mixed = part if mixed is None else mixed + part
    chosen = jnp.concatenate(maps + [mixed], axis=0).astype(BF16)
    slots = chosen.shape[0]
    held_here = dot(chosen, tokens_held(counts, tails, rows, tokens // PAGE).astype(BF16))
    penalty = hide_foreign(held_here, order, tokens)
    for copy in waits[:4]:
        copy.wait()
    newest = dot(chosen, new_kv[...]).astype(BF16)
    hidden[...] = dot(chosen, residual[...])
    squares = [jnp.zeros((slots, HD), F32)]

    def query_of(head):
        picked = dot(chosen, queries[:, head * group * HD : (head + 1) * group * HD])
        return jnp.concatenate([picked[:, g * HD : (g + 1) * HD] for g in range(group)], axis=0).astype(BF16)

    def finish(columns, attended):
        part = hidden[:, columns] + attended
        hidden[:, columns] = part * gain[:, columns]
        squares[0] = squares[0] + part * part

    attend(query_of, newest, pool, penalty, waits[4:], finish)

    sums = jnp.sum(squares[0], axis=1, keepdims=True) + jnp.zeros((slots, LANES), F32)
    upper = iota((LO, 1), 0) < 4
    tail_rows, tail_sums = hidden[hosted * LO :, :], sums[hosted * LO :]
    lane = iota((LO, LANES), 1)
    by_expert = []
    for expert in range(hosted):

        def spread(first, second):
            if expert == 0:
                return jnp.where(upper, first, pltpu.roll(second, 4, 0))
            return jnp.where(upper, pltpu.roll(first, 4, 0), second)

        low = hidden[expert * LO : (expert + 1) * LO, :]
        mix = spread(tail_rows[:, :QUARTER], tail_rows[:, QUARTER:])
        extra = jnp.zeros((LO, LANES), F32)
        pieces = split_three(sums[expert * LO : (expert + 1) * LO]) + split_three(spread(tail_sums, tail_sums))
        for at, piece in enumerate(pieces):
            extra = jnp.where(lane == at, piece, extra)
        by_expert.append(jnp.concatenate([low, mix, extra], axis=1))
    first_half = lax.axis_index("expert") == 0
    extra_at = SLOT_COLS + LANES
    mine = jnp.where(first_half, by_expert[0], by_expert[1])
    kept[:, :extra_at] = jnp.concatenate([mine, jnp.zeros_like(mine)], axis=0).astype(BF16)
    other[...] = jnp.where(first_half, by_expert[1], by_expert[0]).astype(BF16)

    entries = mig_pages.shape[1]
    page_width = pool.shape[1]
    lane = iota((PAGE, LANES), 1)
    notes = jnp.where(lane == entries, lax.axis_index("attn").astype(F32), 0.0)
    for entry in range(entries):
        start = pl.multiple_of(mig_pages[0, entry] * PAGE, PAGE)
        at = extra_at + entry * page_width
        kept[:, at : at + page_width] = pool[pl.ds(start, PAGE), :]
        notes = jnp.where(lane == entry, mig_dest[0, entry].astype(F32), notes)
    kept[:, extra_at + entries * page_width :] = notes.astype(BF16)


def pack_kernel(kept, theirs, message):
    lane = iota((LO, LANES), 1)
    mine = kept[:, : SLOT_COLS + LANES].astype(F32)[:LO]
    extra = mine[:, SLOT_COLS:] + theirs[:, SLOT_COLS:].astype(F32)
    low_scale = lax.rsqrt(jnp.sum(jnp.where(lane < 3, extra, 0.0), axis=1, keepdims=True) / D + EPSILON)
    mix_sum = jnp.sum(jnp.where((lane >= 3) & (lane < 6), extra, 0.0), axis=1, keepdims=True)
    mix_scale = lax.rsqrt(mix_sum / D + EPSILON)
    first_half = lax.axis_index("expert") == 0
    for columns, scale in ((slice(0, HALF), low_scale), (slice(HALF, SLOT_COLS), mix_scale)):
        a = mine[:, columns] * scale
        b = theirs[:, columns].astype(F32) * scale
        both = jnp.concatenate([jnp.where(first_half, a, b), jnp.where(first_half, b, a)], axis=0)
        message[:, columns] = both.astype(BF16)
    message[:, SLOT_COLS:] = kept[:, SLOT_COLS + LANES :]


def copy_kernel(source, out):
    out[...] = source[...]


def fetch_kernel(source, out, sem):
    copy = pltpu.make_async_copy(source, out, sem)
    copy.start()
    copy.wait()


def ffn_kernel(cut, *refs):
    count = len(refs) // 2 - 3 if cut is None else 1
    pieces = count if cut is None else 2
    blocks, (gate, up, down) = refs[:pieces], refs[pieces : pieces + 3]
    outs = refs[pieces + 3 : pieces + 3 + count]
    low_rows, mix_rows, gate_sum, up_sum = refs[pieces + 3 + count :]
    if cut is None:
        for j in range(count):
            low_rows[16 * j : 16 * j + 16, :] = blocks[j][:, :HALF]
            mix_rows[16 * j : 16 * j + 16, :] = blocks[j][:, HALF:SLOT_COLS]
    else:
        low_rows[...] = blocks[0][:, :HALF]
        mix_rows[:, : cut - HALF] = blocks[0][:, HALF:cut]
        mix_rows[:, cut - HALF :] = blocks[1][:, : SLOT_COLS - cut]

    groups = [(first, min(8, count - first)) for first in range(0, count, 8)]
    width = gate.shape[1]
    for q in range(4):
        part = slice(q * QUARTER, (q + 1) * QUARTER)
        within = slice((q % 2) * QUARTER, (q % 2 + 1) * QUARTER)
        for first, size in groups:
            at, span = 16 * first, 16 * size
            row = iota((span, 1), 0) % 16
            low_here, mix_here = (row // 8) == q // 2, (row // 4) == q
            left = jnp.concatenate([low_rows[at : at + span, within], mix_rows[at : at + span, :]], axis=0)
            for weight, total in ((gate, gate_sum), (up, up_sum)):
                product = dot(left, weight[part, :])
                low = jnp.where(low_here, product[:span], 0.0)
                mix = jnp.where(mix_here, product[span:], 0.0)
                if q == 0:
                    total[0, at : at + span, :] = low
                    total[1, at : at + span, :] = mix
                else:
                    total[0, at : at + span, :] += low
                    total[1, at : at + span, :] += mix

    def fold(total, at, size):
        low, mix = [
            jnp.sum(total[k, at : at + 16 * size, :].reshape(size, 2, 8, width), axis=1).reshape(8 * size, width)
            for k in range(2)
        ]
        lower = iota((8 * size, 1), 0) % 8 < 4
        other = jnp.where(lower, pltpu.roll(mix, 8 * size - 4, 0), pltpu.roll(mix, 4, 0))
        return low, mix + other

    first_rows = iota((8, 1), 0) < 4
    for first, size in groups:
        at = 16 * first
        pieces = [jax.nn.silu(g) * u for g, u in zip(fold(gate_sum, at, size), fold(up_sum, at, size))]
        active = jnp.concatenate([p.reshape(size, 8, width) for p in pieces], axis=1)
        active = active.reshape(16 * size, width).astype(BF16)
        quarters = [dot(active, down[:, q * QUARTER : (q + 1) * QUARTER]) for q in range(4)]
        for j in range(size):
            out = outs[first + j]
            low_at, mix_at = slice(16 * j, 16 * j + 8), slice(16 * j + 8, 16 * j + 16)
            for part in range(2):
                both = jnp.concatenate([quarters[part][low_at], quarters[2 + part][low_at]], axis=0)
                out[:, part * QUARTER : (part + 1) * QUARTER] = both.astype(BF16)
            both = jnp.concatenate(
                [jnp.where(first_rows, quarters[k][mix_at], quarters[k + 1][mix_at]) for k in (0, 2)], axis=0
            )
            out[:, HALF:] = both.astype(BF16)


def arrive_kernel(n, cut, page_width, *refs):
    blocks, (arrived, board, board_smem, sem) = refs[: n + 1], refs[n + 1 :]
    entries = arrived.shape[0]
    notes_at = SLOT_COLS + entries * page_width
    heads = [block[:, notes_at:].astype(F32)[0:1] for block in blocks[: n - 1]]
    heads.append(blocks[n][:, notes_at - cut :].astype(F32)[0:1])
    notes = jnp.concatenate(heads, axis=0)
    lane = iota((n, LANES), 1)
    match = (notes == lax.axis_index("attn").astype(F32)) & (lane < entries)
    named = jnp.max(jnp.where(match, 1.0, 0.0), axis=1, keepdims=True)
    source = jnp.sum(jnp.where(lane == entries, notes, 0.0), axis=1, keepdims=True)
    earlier = to_row(source, n) < source
    rank = jnp.sum(jnp.where(earlier, to_row(named, n), 0.0), axis=1, keepdims=True)
    table = jnp.where(match, rank, -1.0)
    if n * entries <= 32:
        pages = [jnp.zeros((PAGE, page_width), F32)] * entries
        for j in range(n):
            block, shift = (blocks[j], 0) if j < n - 1 else (blocks[n], cut)
            for entry in range(entries):
                at = SLOT_COLS + entry * page_width - shift
                page = block[:, at : at + page_width].astype(F32)
                place = jnp.broadcast_to(table[j : j + 1, entry : entry + 1], page.shape)
                pages = [jnp.where(place == float(slot), page, old) for slot, old in enumerate(pages)]
        for slot in range(entries):
            arrived[slot] = pages[slot].astype(BF16)
        return
    board[...] = table.astype(jnp.int32)
    copy = pltpu.make_async_copy(board, board_smem, sem)
    copy.start()
    arrived[...] = jnp.zeros_like(arrived)
    copy.wait()
    for j in range(n):
        block, shift = (blocks[j], 0) if j < n - 1 else (blocks[n], cut)
        for entry in range(entries):
            slot = board_smem[j, entry]
            at = SLOT_COLS + entry * page_width - shift

            @pl.when((slot >= 0) & (slot < entries))
            def _():
                arrived[slot] = block[:, at : at + page_width]


def gather_kernel(core, own, arrived, jumped, out):
    extra = jnp.where(lax.axis_index("expert") == core, jumped[...].astype(F32), 0.0)
    out[...] = (own[...].astype(F32) + arrived[...].astype(F32) + extra).astype(BF16)


def finish_kernel(own, from_left, from_right, mine, other):
    total = own[...].astype(F32) + from_left[...].astype(F32) + from_right[...].astype(F32)
    first_half = lax.axis_index("expert") == 0
    top, bottom = total[:LO], total[LO:]
    mine[...] = jnp.where(first_half, top, bottom).astype(BF16)
    other[...] = jnp.where(first_half, bottom, top).astype(BF16)


def combine_kernel(hosted, hidden, mine, theirs, routes, gates, layer_out):
    rows = hidden.shape[0]
    first_half = lax.axis_index("expert") == 0
    a, b = mine[...].astype(F32), theirs[...].astype(F32)
    by_expert = [jnp.where(first_half, a, b).astype(BF16), jnp.where(first_half, b, a).astype(BF16)]
    row_a, row_b = iota((rows, rows), 0), iota((rows, rows), 1)
    terms = [[], []]
    for expert in range(hosted):
        member = members(routes[...], expert)
        share = jnp.sum(jnp.where(routes[...] == expert, gates[...], 0.0), axis=0, keepdims=True)
        share = to_column(share, rows)
        rank = jnp.sum(jnp.where(row_b <= row_a, member, 0.0), axis=1, keepdims=True) - 1.0
        rank = jnp.where(to_column(member, rows) > 0.0, rank, -2.0)
        low = jnp.where(rank == iota((rows, LO), 1).astype(F32), 1.0, 0.0).astype(BF16)
        for part in range(2):
            columns = slice(part * QUARTER, (part + 1) * QUARTER)
            mix = jnp.where(rank == mix_slots((rows, LO), 1, part), 1.0, 0.0).astype(BF16)
            value = dot(low, by_expert[expert][:, columns]) + dot(mix, by_expert[expert][:, HALF:])
            terms[part].append(share * value)
    for part in range(2):
        columns = slice(part * QUARTER, (part + 1) * QUARTER)
        layer_out[:, columns] = (hidden[:, columns] + (terms[part][0] + terms[part][1])).astype(BF16)


def call(kernel, outs, in_specs, args, scratch=(), flops=0, bytes_accessed=0, vmem=16 << 20):
    many = isinstance(outs, (list, tuple))
    return pl.pallas_call(
        kernel,
        out_shape=outs,
        in_specs=in_specs,
        out_specs=[VMEM] * len(outs) if many else VMEM,
        scratch_shapes=list(scratch),
        compiler_params=pltpu.CompilerParams(vmem_limit_bytes=vmem),
        cost_estimate=pl.CostEstimate(flops=flops, bytes_accessed=bytes_accessed, transcendentals=0),
    )(*args)


def ring_order(n):
    return [0, 2, 4, 6, 7, 5, 3, 1] if n == 8 else list(range(n))


def fetch_weight(shape, weight):
    return call(
        fetch_kernel,
        shape(weight.shape, BF16),
        [HBM],
        (weight,),
        scratch=(pltpu.SemaphoreType.DMA,),
        bytes_accessed=6_400_000,
    )


def add(a, b):
    return (a.astype(F32) + b.astype(F32)).astype(BF16)


def per_device(
    n,
    hosted,
    queries,
    new_kv,
    kv_pool,
    page_counts,
    tail_tokens,
    page_order,
    residual,
    norm_gain,
    routes,
    route_gates,
    w_gate,
    w_up,
    w_down,
    mig_pages,
    mig_dest,
):
    rows, width = queries.shape
    page_width = kv_pool.shape[2]
    entries = mig_pages.shape[1]
    pool = kv_pool.reshape(-1, page_width)
    around = ring_order(n)
    right = [(around[i], around[(i + 1) % n]) for i in range(n)]
    left = [(b, a) for a, b in right]
    reach = n // 2 - 1
    jump = [(around[i] * hosted, around[(i + reach) % n] * hosted + 1) for i in range(n)]
    jump += [(around[i] * hosted + 1, around[(i - reach) % n] * hosted) for i in range(n)]
    swap = [(0, 1), (1, 0)]
    shape = jax.ShapeDtypeStruct

    moved_cols = entries * page_width + LANES
    lengths = (page_counts, tail_tokens.reshape(1, -1), page_order)
    spaces = {mig_pages.shape: pltpu.SMEM}

    def attention(kernel, outs, sources, scratch, flops):
        held = [spaces.get(x.shape, pltpu.VMEM)(x.shape, x.dtype) for x in sources]
        sems = pltpu.SemaphoreType.DMA((len(sources) + page_width // (2 * HD),))
        return call(
            kernel,
            outs,
            [HBM] * len(sources),
            sources,
            scratch=held + scratch + [sems],
            flops=flops,
            bytes_accessed=3_500_000,
            vmem=60 << 20,
        )

    kept, other = attention(
        functools.partial(slots_kernel, hosted),
        [shape((2 * LO, SLOT_COLS + LANES + moved_cols), BF16), shape((LO, SLOT_COLS + LANES), BF16)],
        (*lengths, routes.T, mig_pages, mig_dest, queries, new_kv, residual, norm_gain.reshape(1, -1), pool),
        [pltpu.VMEM((2 * CAP, width), F32)],
        400_000_000,
    )
    tie = lax.optimization_barrier
    theirs = lax.ppermute(other, "expert", swap)
    kept = call(copy_kernel, shape(kept.shape, BF16), [VMEM], (kept,), bytes_accessed=3_000_000)
    theirs, kept = tie((theirs, kept))
    message = call(
        pack_kernel,
        shape((2 * LO, SLOT_COLS + moved_cols), BF16),
        [VMEM] * 2,
        (kept, theirs),
        flops=500_000,
        bytes_accessed=500_000,
    )

    far = n // 2
    cut = HALF + 3 * LANES
    fetch = functools.partial(fetch_weight, shape)
    from_left, from_right = [message], [message]
    weights, stored = [], [w_gate[0], w_up[0], w_down[0]]
    for step in range(far):
        a, b = from_left[-1], from_right[-1]
        if step == far - 1:
            a, b = a[:, :cut], b[:, cut:]
        a, b = lax.ppermute(a, "attn", right), lax.ppermute(b, "attn", left)
        if step == 0:
            hidden = attention(
                hidden_kernel,
                shape((rows, width), F32),
                (*lengths, queries, new_kv, residual, pool),
                [],
                4_000_000_000,
            )
            b, hidden = tie((b, hidden))
        else:
            for weight in {1: stored[:1], 2: stored[1:]}.get(step, []):
                weights.append(fetch(weight))
                if step == 2:
                    b, weights[-1] = tie((b, weights[-1]))
                else:
                    b, weights[-1] = tie((b, weights[-1]))
        from_left.append(a)
        from_right.append(b)
    last_a, last_b = from_left.pop(), from_right.pop()
    blocks = [message] + from_left[1:] + from_right[1:]
    ff = w_gate.shape[2]

    def feed_forward(pieces, count, cut):
        return call(
            functools.partial(ffn_kernel, cut),
            [shape((2 * LO, SLOT_COLS), BF16)] * count,
            [VMEM] * (len(pieces) + 3),
            (*pieces, *weights),
            scratch=(
                pltpu.VMEM((16 * count, HALF), BF16),
                pltpu.VMEM((16 * count, QUARTER), BF16),
                pltpu.VMEM((2, 16 * count, ff), F32),
                pltpu.VMEM((2, 16 * count, ff), F32),
            ),
            flops=2_000_000_000,
            bytes_accessed=8_000_000,
        )

    outs = list(feed_forward(blocks, n - 1, None))
    to_left = {k: outs[k] for k in range(1, far)}
    to_right = {k: outs[far - 1 + k] for k in range(1, far)}
    going_right = going_left = jumped = None

    def gather(core, *terms):
        return call(
            functools.partial(gather_kernel, core),
            shape((2 * LO, SLOT_COLS), BF16),
            [VMEM] * 3,
            terms,
            flops=300_000,
            bytes_accessed=600_000,
        )

    for k in range(far - 1, 0, -1):
        send_right, send_left = to_right[k], to_left[k]
        if k == 1:
            send_right, send_left = gather(0, send_right, going_right, jumped), gather(1, send_left, going_left, jumped)
        elif k < far - 1:
            send_right, send_left = add(send_right, going_right), add(send_left, going_left)
        going_right = lax.ppermute(send_right, "attn", right)
        going_left = lax.ppermute(send_left, "attn", left)
        if k == far - 1:
            (opposite,) = feed_forward((last_a, last_b), 1, cut)
            going_right, opposite = tie((going_right, opposite))
            jumped = lax.ppermute(lax.ppermute(opposite, ("attn", "expert"), jump), "expert", swap)
        if k == far - 2:
            arrived = call(
                functools.partial(arrive_kernel, n, cut, page_width),
                shape((entries, PAGE, page_width), BF16),
                [VMEM] * (n + 1),
                (*blocks, last_a, last_b),
                scratch=(
                    pltpu.VMEM((n, LANES), jnp.int32),
                    pltpu.SMEM((n, LANES), jnp.int32),
                    pltpu.SemaphoreType.DMA,
                ),
                flops=100_000,
                bytes_accessed=2_000_000,
            )
            going_left, arrived = tie((going_left, arrived))
    kept, other_half = call(
        finish_kernel,
        [shape((LO, SLOT_COLS), BF16)] * 2,
        [VMEM] * 3,
        (outs[0], going_right, going_left),
        flops=500_000,
        bytes_accessed=600_000,
    )
    returned = lax.ppermute(other_half, "expert", swap)
    layer_out = call(
        functools.partial(combine_kernel, hosted),
        shape((rows, width), BF16),
        [VMEM] * 5,
        (hidden, kept, returned, routes.T, route_gates.T),
        flops=20_000_000,
        bytes_accessed=800_000,
    )
    return layer_out, arrived


def solution(mesh):
    n, hosted = mesh.shape["attn"], mesh.shape["expert"]
    return jax.shard_map(
        functools.partial(per_device, n, hosted),
        mesh=mesh,
        in_specs=(
            P(("groups", "attn"), "expert"),
            P(("groups", "attn"), "expert"),
            P(("groups", "attn"), None, "expert"),
            P(("groups", "attn"), None),
            P(("groups", "attn")),
            P(("groups", "attn"), None),
            P(("groups", "attn"), "expert"),
            P("expert"),
            P(("groups", "attn"), None),
            P(("groups", "attn"), None),
            P("expert", None, "attn"),
            P("expert", None, "attn"),
            P("expert", "attn", None),
            P(("groups", "attn"), None),
            P(("groups", "attn"), None),
        ),
        out_specs=(P(("groups", "attn"), "expert"), P(("groups", "attn"), None, "expert")),
        check_vma=False,
    )
```
